32 devices in a mesh: dp: 8 (over y, x, core), seq: 4 (over z).
Axes of the slice: x: 2, y: 2, z: 4, core: 2. Of those that a mesh axis runs over, the one named last changes fastest.
Arguments:
- inputs: bfloat16 [16, 1024, 768], P('dp', 'seq'), may hold values from -6 to 6
- cotangent: bfloat16 [16, 1024, 768], P('dp', 'seq'), may hold values from -6 to 6
- time_table: bfloat16 [2000, 768], replicated, may hold values from -6 to 6
- timesteps: int32 [16], P('dp'), may hold values from 0 to 1999
- buckets: int32 [16], P('dp'), may hold values from 0 to 7
- mixer_weight: bfloat16 [768, 2304], replicated, may hold values from -0.3125 to 0.3125
- output_weight: bfloat16 [768, 768], replicated, may hold values from -0.75 to 0.75
- up_weight: bfloat16 [768, 3072], replicated, may hold values from -0.21875 to 0.21875
- down_weight: bfloat16 [3072, 768], replicated, may hold values from -0.109375 to 0.109375
- norm_gain: bfloat16 [2, 768], replicated, may hold values from 0.5 to 1.5
- norm_shift: bfloat16 [2, 768], replicated, may hold values from -3 to 3
- output_bias: bfloat16 [2, 768], replicated, may hold values from -3 to 3
- up_bias: bfloat16 [3072], replicated, may hold values from -4 to 4
Outputs:
- layer_out: bfloat16 [16, 1024, 768], P('dp', 'seq')
- input_grad: float32 [16, 1024, 768], P('dp', 'seq')
- mixer_grad: float32 [768, 2304], P('dp')
- output_grad: float32 [768, 768], P('dp')
- up_grad: float32 [768, 3072], P('dp')
- down_grad: float32 [3072, 768], P('dp')
- gain_grad: float32 [2, 768], replicated
- shift_grad: float32 [2, 768], replicated
- bias_grad: float32 [2, 768], replicated
- up_bias_grad: float32 [3072], replicated
- table_grad: float32 [2000, 768], P(None, 'dp')
- bucket_norms: float32 [8], replicated
- bucket_counts: float32 [8], replicated
The draws below stay inside these ranges and needn't reach their ends.
All inputs are finite; a program needn't handle non-finite values.
Results may differ from the reference program's by a relative error of at most 0.012.
Values may be sent and summed in bfloat16 or wider, within the bound.
A program may use at most 192 MiB of HBM per device.

```python
import math
import jax
import jax.numpy as jnp
import numpy as np
from jax import lax

D = 768
HEADS = 12
HEAD_SIZE = 64
FF = 3072
STEPS = 2000
BUCKETS = 8
LENGTH = 1024
SEQUENCES = 16


def set_ends(values, key, smallest, high):
    index_at = [jax.random.randint(jax.random.fold_in(key, axis), (), 0, length) for axis, length in enumerate(values.shape)]
    main_axis = values.shape.index(max(values.shape))
    next_to = index_at[:main_axis] + [(index_at[main_axis] + 1) % values.shape[main_axis]] + index_at[main_axis + 1:]
    return values.at[tuple(index_at)].set(smallest).at[tuple(next_to)].set(high)


def spiked(values, rng, source, target, shards_of, factor):
    owner, partner = [(jnp.arange(values.shape[axis_at]) // (values.shape[axis_at] // shards_of)).reshape([-1 if axis == axis_at else 1 for axis in range(values.ndim)]) for axis_at in (source, target)]
    chosen = jax.random.permutation(rng, shards_of)[partner]
    strong = (owner == chosen) | (owner == (partner + shards_of // 2) % shards_of)
    return jnp.where(strong, factor * values, values)


def block_scale(key, extent, split, low, largest):
    gain = 1.0
    for position, blocks in split:
        steps = jax.random.uniform(jax.random.fold_in(jax.random.fold_in(key, 6), position), (blocks,), jnp.float32, low / len(split), largest / len(split))
        gain = gain * jnp.repeat(jnp.exp(steps), extent[position] // blocks).reshape((-1,) + (1,) * (len(extent) - 1 - position))
    return gain


def cumulative_ranks(amount, slope):
    weights = [(1 << 20) // math.isqrt(standing ** slope) + 1 for standing in range(1, amount + 1)]
    deviation = 1 + sum(weights) // (1 << 30)
    return np.cumsum(np.array([max(1, weight // deviation) for weight in weights]))


def ranked_ids(key, dims, amount, skew):
    grid = cumulative_ranks(amount, skew)
    pick = jax.random.randint(jax.random.fold_in(key, 1), dims, 0, int(grid[amount - 1]))
    standing = jnp.searchsorted(jnp.asarray(grid, jnp.int32), pick, side="right")
    return jax.random.permutation(jax.random.fold_in(key, 2), amount)[standing].astype(jnp.int32)


def gaussian(stream_key, shape, width, reach, shards=(), held_as=jnp.bfloat16):
    entries = width * jax.random.normal(stream_key, shape, jnp.float32)
    if shards:
        entries = entries * block_scale(stream_key, shape, shards, -0.22, 0.18)
    return jnp.clip(entries, -reach, reach).astype(held_as)


def gaussian_with(key, dims, scale, reach, cuts, heavy, kind=jnp.bfloat16):
    drawn = scale * jax.random.normal(key, dims, jnp.float32)
    if cuts:
        drawn = drawn * block_scale(key, dims, cuts, -0.22, 0.18)
    return jnp.clip(spiked(drawn, jax.random.fold_in(key, 3), *heavy), -reach, reach).astype(kind)


def setup_inputs(seed: int = 0) -> dict:
    arg_keys = jax.random.split(jax.random.key(seed), 14)
    return {
        "inputs": gaussian_with(arg_keys[0], (SEQUENCES, LENGTH, D), 1.0, 6.0, ((0, 8), (1, 4)), (0, 2, 8, 2.0)),
        "cotangent": gaussian(arg_keys[1], (SEQUENCES, LENGTH, D), 1.0, 6.0, ((0, 8), (1, 4))),
        "time_table": gaussian(arg_keys[2], (STEPS, D), 1.0, 6.0),
        "timesteps": set_ends(ranked_ids(arg_keys[3], (SEQUENCES,), STEPS, 2), jax.random.fold_in(arg_keys[3], 3), 0, STEPS - 1).astype(jnp.int32),
        "buckets": set_ends(jax.random.randint(arg_keys[4], (SEQUENCES,), 0, BUCKETS), jax.random.fold_in(arg_keys[4], 1), 0, BUCKETS - 1).astype(jnp.int32),
        "mixer_weight": gaussian(arg_keys[5], (D, 3 * D), (D // 2) ** -0.5, 0.3125),
        "output_weight": gaussian(arg_keys[6], (D, D), HEAD_SIZE ** -0.5, 0.75),
        "up_weight": gaussian(arg_keys[7], (D, FF), D ** -0.5, 0.21875),
        "down_weight": gaussian(arg_keys[8], (FF, D), FF ** -0.5, 0.109375),
        "norm_gain": jnp.clip(1.0 + 0.1 * jax.random.normal(arg_keys[9], (2, D), jnp.float32), 0.5, 1.5).astype(jnp.bfloat16),
        "norm_shift": gaussian(arg_keys[10], (2, D), 0.3, 3.0),
        "output_bias": gaussian(arg_keys[11], (2, D), 0.3, 3.0),
        "up_bias": gaussian(arg_keys[12], (FF,), 0.5, 4.0),
    }


EPS = 1e-05
HIGH = lax.Precision.HIGHEST

@jax.custom_vjp
def low(v):
    return lax.optimization_barrier(v.astype(jnp.bfloat16)).astype(jnp.float32)

@jax.custom_vjp
def low_back(v):
    return v

def low_keep(v):
    return (low(v), None)

def low_pass(kept, grad):
    return (grad,)

def back_keep(v):
    return (v, None)

def back_low(kept, grad):
    return (low(grad),)
low.defvjp(low_keep, low_pass)
low_back.defvjp(back_keep, back_low)

def product(left_side, right_side):
    return jnp.dot(left_side, right_side, precision=HIGH, preferred_element_type=jnp.float32)

def layer_norm(values, gain_row, shift_row):
    centre = lax.optimization_barrier(jnp.mean(values, axis=-1, keepdims=True))
    centred = values - centre
    spread = lax.optimization_barrier(jnp.mean(centred * centred, axis=-1, keepdims=True))
    return centred * lax.rsqrt(spread + EPS) * gain_row + shift_row

def one_head(packed):
    query_rows = packed[:, 0]
    key_rows = packed[:, 1]
    value_rows = packed[:, 2]
    scores = low_back(product(query_rows, key_rows.T) * (1.0 / math.sqrt(HEAD_SIZE)))
    softmax_rows = low(jax.nn.softmax(scores, axis=-1))
    return product(softmax_rows, value_rows)

def block(weight_set, rows_in, table, steps_now):
    mixer, output, upper, lower, gains, shifts, biases, up_vector = weight_set
    group_size = rows_in.shape[0]
    summed_in = rows_in + table[steps_now][:, None, :]
    low_one = low(layer_norm(summed_in, gains[0], shifts[0])).reshape(group_size * LENGTH, D)
    projected = low(low_back(product(low_one, mixer)))
    packed = projected.reshape(group_size, LENGTH, HEADS, 3, HEAD_SIZE).transpose(0, 2, 1, 3, 4)
    packed = packed.reshape(group_size * HEADS, LENGTH, 3, HEAD_SIZE)
    heads_out = lax.map(jax.checkpoint(one_head), packed)
    mixed_tokens = heads_out.reshape(group_size, HEADS, LENGTH, HEAD_SIZE).transpose(0, 2, 1, 3)
    mixed_tokens = low(low_back(mixed_tokens.reshape(group_size * LENGTH, D)))
    branch = low_back(product(mixed_tokens, output) + biases[0])
    middle = summed_in.reshape(group_size * LENGTH, D) + branch
    low_two = low(layer_norm(middle, gains[1], shifts[1]))
    raised = low_back(product(low_two, upper) + up_vector)
    hidden = low(jax.nn.gelu(raised, approximate=False))
    final_rows = middle + low_back(product(hidden, lower) + biases[1])
    return final_rows.reshape(group_size, LENGTH, D)

def reference(inputs, cotangent, time_table, timesteps, buckets, mixer_weight, output_weight, up_weight, down_weight, norm_gain, norm_shift, output_bias, up_bias):
    weights = tuple((member.astype(jnp.float32) for member in (mixer_weight, output_weight, up_weight, down_weight, norm_gain, norm_shift, output_bias, up_bias)))
    table = time_table.astype(jnp.float32)
    group_size = math.gcd(SEQUENCES, max(1, 4096 // LENGTH))
    group_count = SEQUENCES // group_size
    inputs_grouped = inputs.astype(jnp.float32).reshape(group_count, group_size, LENGTH, D)
    cot_grouped = cotangent.astype(jnp.float32).reshape(group_count, group_size, LENGTH, D)
    steps_grouped = timesteps.astype(jnp.int32).reshape(group_count, group_size)

    def one_group(running, sliced):
        rows_in, cot_in, steps_now = sliced

        def apply_block(weight_set, rows_arg, table_arg):
            return block(weight_set, rows_arg, table_arg, steps_now)
        final_rows, pull_back = jax.vjp(apply_block, weights, rows_in, table)
        grad_weights, grad_rows, grad_table = pull_back(cot_in)
        weight_sums, table_sum = running
        return ((jax.tree.map(jnp.add, weight_sums, grad_weights), table_sum + grad_table), (final_rows, grad_rows))
    initial = (jax.tree.map(jnp.zeros_like, weights), jnp.zeros_like(table))
    (weight_sums, table_sum), (final_all, grad_all) = lax.scan(one_group, initial, (inputs_grouped, cot_grouped, steps_grouped))
    final_all = final_all.reshape(SEQUENCES, LENGTH, D)
    grad_all = grad_all.reshape(SEQUENCES, LENGTH, D)
    square_mean = lax.optimization_barrier(jnp.mean(final_all * final_all, axis=(1, 2)))
    bucket_hits = (buckets[:, None] == jnp.arange(BUCKETS, dtype=jnp.int32)[None, :]).astype(jnp.float32)
    return (final_all.astype(jnp.bfloat16), grad_all, weight_sums[0], weight_sums[1], weight_sums[2], weight_sums[3], weight_sums[4], weight_sums[5], weight_sums[6], weight_sums[7], table_sum, lax.optimization_barrier(jnp.sum(bucket_hits * square_mean[:, None], axis=0)), lax.optimization_barrier(jnp.sum(bucket_hits, axis=0)))
```

```python
import functools
import math

import jax
import jax.numpy as jnp
from jax import lax
from jax.experimental import pallas as pl
from jax.experimental.pallas import tpu as pltpu
from jax.sharding import PartitionSpec as P

HEADS = 12
HEAD_SIZE = 64
PAIRS = HEADS // 2
PAIR = 2 * HEAD_SIZE
STEPS = 2000
BUCKETS = 8
EPS = 1e-05

BF = jnp.bfloat16
F32 = jnp.float32
MESH = pl.DeviceIdType.MESH


def mm(a, b):
    return lax.dot_general(a, b, (((1,), (0,)), ((), ())), preferred_element_type=F32)


def mm_nt(a, b):
    return lax.dot_general(a, b, (((1,), (1,)), ((), ())), preferred_element_type=F32)


def mm_tn(a, b):
    return lax.dot_general(a, b, (((0,), (0,)), ((), ())), preferred_element_type=F32)


def iota(shape, axis):
    return lax.broadcasted_iota(jnp.int32, shape, axis)


def place():
    d, z = lax.axis_index("dp"), lax.axis_index("seq")
    return d, z, lax.rem(d, 2), lax.div(d, 2)


def column_peers():
    d, z, c, k = place()
    found = []
    for off in range(1, 8):
        m = lax.rem(c * 4 + z + off, 8)
        found.append((2 * k + lax.div(m, 4), lax.rem(m, 4)))
    return found


def greet(ids):
    barrier = pltpu.get_barrier_semaphore()
    for one in ids:
        pl.semaphore_signal(barrier, inc=1, device_id=one, device_id_type=MESH)
    pl.semaphore_wait(barrier, len(ids))


def swap_part(i):
    d, z, c, k = place()
    core, chip = lax.div(z, 2), 2 * c + i
    return core, chip, jnp.logical_and(core == c, chip == z), 2 * k + core


def swap_start(source, target, send, recv):
    z = lax.axis_index("seq")
    slot = lax.rem(z, 2)
    for i in range(2):
        core, chip, own, there = swap_part(i)

        @pl.when(own)
        def _():
            pltpu.make_async_copy(source(i), target(slot), recv.at[slot]).start()

        @pl.when(jnp.logical_not(own))
        def _():
            pltpu.make_async_remote_copy(
                source(i), target(slot), send.at[i], recv.at[slot],
                device_id=(there, chip), device_id_type=MESH,
            ).start()


def swap_wait(target, recv, s):
    pltpu.make_async_copy(target(s), target(s), recv.at[s]).wait()


def swap_sent(source, target, send, recv):
    for i in range(2):
        core, chip, own, there = swap_part(i)

        @pl.when(jnp.logical_not(own))
        def _():
            pltpu.make_async_remote_copy(
                source(i), target(i), send.at[i], recv.at[i],
                device_id=(there, chip), device_id_type=MESH,
            ).wait_send()


def forward_kernel(
    ts, x, cot, table, wm, wo, wu, wd, gains, shifts, biases, upb,
    lout, s_out, low1_out, q_out, kv_out, ls_out, do_out, dt_out, gm_out, g_out, small_out,
    xr, cr, embs, embr, tabv, wmv, wov, wuv, wdv, sv, low1, q2, kv, mixed, ls, lst,
    mid, low2, low2t, hid, rl, gf, lov, dov, dtv, gmv, gv, small, upg, sqv,
    xsend, xrecv, csend, crecv, esend, erecv, ksend, krecv, wsem, osem,
):
    d, z, c, k = place()
    toks, width = xr.shape
    part = toks // 2
    hidden_width = wuv.shape[1]

    def fetch(i, src, dst):
        return pltpu.make_async_copy(src, dst, wsem.at[i])

    def put(i, src, dst):
        return pltpu.make_async_copy(src, dst, osem.at[i])

    fetch(0, table, tabv).start()
    greet(column_peers())
    x_at = lambda s: xr.at[pl.ds(pl.multiple_of(s * part, part), part)]
    c_at = lambda s: cr.at[pl.ds(pl.multiple_of(s * part, part), part)]
    swap_start(lambda i: x.at[i], x_at, xsend, xrecv)
    fetch(1, wm, wmv).start()
    fetch(2, wo, wov).start()
    fetch(3, wu, wuv).start()
    fetch(4, wd, wdv).start()
    fetch(0, table, tabv).wait()
    row, col = iota((16, tabv.shape[0]), 0), iota((16, tabv.shape[0]), 1)
    wanted = jnp.where(row == 0, ts[0], ts[1])
    picked = mm(jnp.where(jnp.logical_and(col == wanted, row < 2), 1.0, 0.0).astype(BF), tabv[...])
    for i in range(2):
        embs[i] = jnp.broadcast_to(picked[i : i + 1], (16, width)).astype(BF)
    swap_start(lambda i: embs.at[i], lambda s: embr.at[s], esend, erecv)
    for s in range(2):
        swap_wait(lambda s: embr.at[s], erecv, s)
    for s in range(2):
        swap_wait(x_at, xrecv, s)
    swap_start(lambda i: cot.at[i], c_at, csend, crecv)
    gain0, shift0 = gains[0:1, :].astype(F32), shifts[0:1, :].astype(F32)
    gain1, shift1 = gains[1:2, :].astype(F32), shifts[1:2, :].astype(F32)
    bias0, bias1 = biases[0:1, :].astype(F32), biases[1:2, :].astype(F32)

    for s in range(2):
        emb = embr[s][0:1, :].astype(F32)

        @pl.loop(0, part // 128)
        def _(b):
            rows = pl.ds(pl.multiple_of(s * part + b * 128, 128), 128)
            v = xr[rows, :].astype(F32) + emb
            cen = v - jnp.mean(v, axis=-1, keepdims=True)
            inv = lax.rsqrt(jnp.mean(cen * cen, axis=-1, keepdims=True) + EPS)
            sv[rows, :] = v
            low1[rows, :] = (cen * inv * gain0 + shift0).astype(BF)

    put(0, sv, s_out).start()
    put(1, low1, low1_out).start()

    mine = pl.ds(pl.multiple_of(c * toks, toks), toks)
    partner = d + 1 - 2 * c

    def kv_copy(p):
        return pltpu.make_async_remote_copy(
            kv.at[p, :, mine], kv.at[p, :, mine], ksend.at[p], krecv.at[p],
            device_id=(partner, z), device_id_type=MESH,
        )

    fetch(1, wm, wmv).wait()
    low_half = iota((1, PAIR), 1) < HEAD_SIZE

    @pl.loop(0, PAIRS)
    def _(p):
        cols = pl.ds(pl.multiple_of(p * 3 * PAIR, PAIR), 3 * PAIR)
        res = mm(low1[...], wmv[:, cols])
        t0, t1, t2 = res[:, :PAIR], res[:, PAIR : 2 * PAIR], res[:, 2 * PAIR :]
        q2[p] = (jnp.where(low_half, t0, t1).astype(BF) * 0.125).astype(BF)
        kv[p, 0, mine, :] = pltpu.roll(jnp.where(low_half, t2, t0), HEAD_SIZE, 1).astype(BF)
        kv[p, 1, mine, :] = jnp.where(low_half, t1, t2).astype(BF)
        kv_copy(p).start()

    put(2, q2, q_out).start()

    lane = iota((1, PAIR), 1)
    blk = toks // 2

    @pl.loop(0, PAIRS)
    def _(p):
        kv_copy(p).wait_recv()

        @pl.loop(0, 2)
        def _(b):
            rows = pl.ds(pl.multiple_of(b * blk, blk), blk)
            q = q2[p, rows, :]
            keys, vals = kv[p, 0], kv[p, 1]
            outs, sums = [], []
            for h in range(2):
                own = low_half if h == 0 else jnp.logical_not(low_half)
                s = mm_nt(jnp.where(own, q, jnp.zeros_like(q)), keys)
                top = jnp.max(s, axis=-1, keepdims=True)
                e = jnp.exp(s - top)
                total = jnp.sum(e, axis=-1, keepdims=True)
                outs.append(mm(e.astype(BF), vals) * (1.0 / total))
                sums.append(top + jnp.log(total))
            cols = pl.ds(pl.multiple_of(p * PAIR, PAIR), PAIR)
            mixed[rows, cols] = jnp.where(low_half, outs[0], outs[1]).astype(BF)
            ls[rows, :] = jnp.where(
                lane == 2 * p, sums[0], jnp.where(lane == 2 * p + 1, sums[1], ls[rows, :])
            )

    put(3, kv, kv_out).start()
    lst[...] = ls[...].T
    put(4, lst, ls_out).start()
    fetch(2, wo, wov).wait()

    @pl.loop(0, 2)
    def _(b):
        rows = pl.ds(pl.multiple_of(b * blk, blk), blk)
        v = sv[rows, :] + mm(mixed[rows, :], wov[...]) + bias0
        mid[rows, :] = v
        cen = v - jnp.mean(v, axis=-1, keepdims=True)
        inv = lax.rsqrt(jnp.mean(cen * cen, axis=-1, keepdims=True) + EPS)
        low = cen * inv * gain1 + shift1
        low2[rows, :] = low.astype(BF)

    low2t[...] = low2[...].T
    fetch(3, wu, wuv).wait()
    fetch(4, wd, wdv).wait()
    for s in range(2):
        swap_wait(c_at, crecv, s)
    step = 256

    @pl.loop(0, hidden_width // step)
    def _(j):
        cols = pl.ds(pl.multiple_of(j * step, step), step)
        r = mm(low2[...], wuv[:, cols]) + upb[:, cols].astype(F32)
        back = mm_nt(cr[...], wdv[cols, :])
        half = 0.5 * (1.0 + lax.erf(r * math.sqrt(0.5)))
        bell = jnp.exp(r * r * -0.5) * (1.0 / math.sqrt(2.0 * math.pi))
        hid[:, cols] = (r * half).astype(BF)
        low = (back * (half + r * bell)).astype(BF)
        rl[:, cols] = low
        upg[:, cols] = jnp.sum(low.astype(F32), axis=0, keepdims=True)

    @pl.loop(0, width // step)
    def _(j):
        cols = pl.ds(pl.multiple_of(j * step, step), step)
        fin = mid[:, cols] + mm(hid[...], wdv[:, cols]) + biases[1:2, cols].astype(F32)
        lov[:, cols] = fin.astype(BF)
        sqv[:, cols] = jnp.sum(fin * fin, axis=0, keepdims=True)
        gf[:, cols] = mm_nt(rl[...], wuv[cols, :])

    put(5, lov, lout).start()
    shard = hidden_width // 8
    quarter = shard // 4

    def slot(s):
        return lax.div(s, 4), lax.rem(lax.div(s, 2), 2), lax.rem(s, 2)

    @pl.loop(0, 8)
    def _(s):
        cols = pl.ds(pl.multiple_of(s * shard, shard), shard)
        res = mm_tn(hid[:, cols], cr[...]).astype(BF)
        b2, b1, b0 = slot(s)
        for i in range(4):
            gv[i, b2, b1, b0] = res[i * quarter : (i + 1) * quarter]

    @pl.loop(0, 4)
    def _(j):
        cols = pl.ds(pl.multiple_of(j * width, width), width)
        for h in range(2):
            res = mm(low2t[h * width // 2 : (h + 1) * width // 2, :], rl[:, cols]).astype(BF)
            for i in range(4):
                gv[4 + j, h, i // 2, i % 2] = res[i * quarter : (i + 1) * quarter]

    small[...] = jnp.zeros_like(small)

    @pl.loop(0, toks // 128)
    def _(b):
        rows = pl.ds(pl.multiple_of(b * 128, 128), 128)
        v = mid[rows, :]
        cen = v - jnp.mean(v, axis=-1, keepdims=True)
        inv = lax.rsqrt(jnp.mean(cen * cen, axis=-1, keepdims=True) + EPS)
        unit = cen * inv
        raw = gf[rows, :]
        g = raw * gain1
        centred = (
            g - jnp.mean(g, axis=-1, keepdims=True)
            - unit * jnp.mean(g * unit, axis=-1, keepdims=True)
        )
        ct = cr[rows, :].astype(F32)
        grad = ct + centred * inv
        low = grad.astype(BF)
        gmv[rows, :] = grad
        small[0:1, :] += jnp.sum(raw * unit, axis=0, keepdims=True)
        small[1:2, :] += jnp.sum(raw, axis=0, keepdims=True)
        small[2:3, :] += jnp.sum(low.astype(F32), axis=0, keepdims=True)
        small[3:4, :] += jnp.sum(ct, axis=0, keepdims=True)

    put(6, gmv, gm_out).start()
    for i in range(4):
        small[4 + i : 5 + i, :] = upg[:, i * width : (i + 1) * width]
    small[8:9, :] = sqv[...]

    fold = jnp.where(lax.div(iota((PAIR, width), 1), HEAD_SIZE) == iota((PAIR, width), 0), 1.0, 0.0)
    fold = fold.astype(BF)

    @pl.loop(0, 2)
    def _(b):
        rows = pl.ds(pl.multiple_of(b * blk, blk), blk)
        dout = mm_nt(gmv[rows, :].astype(BF), wov[...]).astype(BF)
        dov[rows, :] = dout
        prod = dout.astype(F32) * mixed[rows, :].astype(F32)
        high = prod.astype(BF)
        rest = (prod - high.astype(F32)).astype(BF)
        dtv[:, rows] = mm_nt(fold, high) + mm_nt(fold, rest)

    put(7, dov, do_out).start()
    put(8, dtv, dt_out).start()
    for h in range(2):
        res = mm_tn(mixed[:, h * width // 2 : (h + 1) * width // 2], gmv[...].astype(BF)).astype(BF)
        for i in range(4):
            gv[8, h, i // 2, i % 2] = res[i * quarter : (i + 1) * quarter]
    put(9, gv, g_out).start()
    put(10, small, small_out).start()

    swap_sent(lambda i: x.at[i], x_at, xsend, xrecv)
    swap_sent(lambda i: cot.at[i], c_at, csend, crecv)
    swap_sent(lambda i: embs.at[i], lambda s: embr.at[s], esend, erecv)

    @pl.loop(0, PAIRS)
    def _(p):
        kv_copy(p).wait_send()

    for i, (src, dst) in enumerate((
        (sv, s_out), (low1, low1_out), (q2, q_out), (kv, kv_out), (lst, ls_out), (lov, lout),
        (gmv, gm_out), (dov, do_out), (dtv, dt_out), (gv, g_out), (small, small_out),
    )):
        put(i, src, dst).wait()


def sds(shape, dtype):
    return jax.ShapeDtypeStruct(shape, dtype)


def run_forward(ts, x, cot, table, wm, wo, wu, wd, gains, shifts, biases, upb):
    seqs, part, width = x.shape
    toks = 2 * part
    ff = wu.shape[1]
    shard = width // 8
    outs = dict(
        lout=sds((toks, width), BF), s=sds((toks, width), F32), low1=sds((toks, width), BF),
        q=sds((PAIRS, toks, PAIR), BF), kv=sds((PAIRS, 2, 2 * toks, PAIR), BF),
        ls=sds((PAIR, toks), F32), do=sds((toks, width), BF), dt=sds((PAIR, toks), F32),
        gm=sds((toks, width), F32), g=sds((9, 2, 2, 2, shard, width), BF), small=sds((16, width), F32),
    )
    vm = lambda shape, dtype: pltpu.VMEM(shape, dtype)
    any_ = pl.BlockSpec(memory_space=pl.ANY)
    vmem = pl.BlockSpec(memory_space=pltpu.VMEM)
    dma = lambda *n: pltpu.SemaphoreType.DMA(n)
    res = pl.pallas_call(
        forward_kernel,
        out_shape=tuple(outs.values()),
        in_specs=[pl.BlockSpec(memory_space=pltpu.SMEM)] + [any_] * 7 + [vmem] * 4,
        out_specs=tuple([any_] * len(outs)),
        scratch_shapes=[
            vm((toks, width), BF), vm((toks, width), BF), vm((2, 16, width), BF), vm((2, 16, width), BF),
            vm(table.shape, BF), vm(wm.shape, BF), vm(wo.shape, BF), vm(wu.shape, BF), vm(wd.shape, BF),
            vm((toks, width), F32), vm((toks, width), BF), vm((PAIRS, toks, PAIR), BF),
            vm((PAIRS, 2, 2 * toks, PAIR), BF), vm((toks, width), BF), vm((toks, PAIR), F32),
            vm((PAIR, toks), F32), vm((toks, width), F32), vm((toks, width), BF), vm((width, toks), BF),
            vm((toks, ff), BF), vm((toks, ff), BF), vm((toks, width), F32), vm((toks, width), BF),
            vm((toks, width), BF), vm((PAIR, toks), F32), vm((toks, width), F32),
            vm((9, 2, 2, 2, shard, width), BF), vm((16, width), F32), vm((1, ff), F32), vm((1, width), F32),
            dma(2), dma(2), dma(2), dma(2), dma(2), dma(2), dma(PAIRS), dma(PAIRS), dma(5), dma(11),
        ],
        compiler_params=pltpu.CompilerParams(
            collective_id=0, has_side_effects=True, vmem_limit_bytes=60 << 20
        ),
        cost_estimate=pl.CostEstimate(flops=16_000_000_000, bytes_accessed=50_000_000, transcendentals=10_000_000),
        name="forward",
    )(ts, x, cot, table, wm, wo, wu, wd, gains, shifts, biases, upb.reshape(1, ff))
    return dict(zip(outs, res))


def flip(index, bit):
    return index + bit - 2 * bit * lax.rem(lax.div(index, bit), 2)


def bit_of(index, bit):
    return lax.rem(lax.div(index, bit), 2)


def axis_bits(size):
    found, bit = [], 1
    while bit < size:
        found.append(bit)
        bit *= 2
    return found


def add_into(dst, src):
    dst[...] = (dst[...].astype(F32) + src[...].astype(F32)).astype(dst.dtype)


class Reduction:
    STAGES = 7

    def __init__(self, index, first, count, kind, refs, outer):
        self.index, self.first, self.count, self.kind = index, first, count, kind
        self.g, self.r0, self.r1, self.r2, self.r3, self.r4, self.f, self.send, self.recv = refs
        d, z, _, _ = place()
        self.b0, self.b1, self.b2 = bit_of(d, outer), bit_of(d, 2 * outer), bit_of(d, 4 * outer)
        self.p0 = (flip(d, outer), z)
        self.p1 = (flip(d, 2 * outer), z)
        self.p2 = (flip(d, 4 * outer), z)
        self.z0, self.z1 = lax.rem(z, 2), lax.div(z, 2)
        self.q0, self.q1 = (d, flip(z, 1)), (d, flip(z, 2))
        rows, cols = self.g.shape[-2] // 2, self.g.shape[-1] // 2
        at = lambda b, n: pl.ds(pl.multiple_of(b * n, n), n)
        self.rows, self.other_rows = at(self.z0, rows), at(1 - self.z0, rows)
        self.cols, self.other_cols = at(self.z1, cols), at(1 - self.z1, cols)
        self.stage = 0

    def copy(self, stage):
        u = pl.ds(self.first, self.count)
        b0, b1, b2 = self.b0, self.b1, self.b2
        if stage == 0:
            src, dst, to = self.g.at[u, :, :, 1 - b0], self.r0.at[u], self.p0
        elif stage == 1 and self.kind == "a":
            src, dst, to = self.g.at[u, :, 1 - b1, b0], self.r1.at[u], self.p1
        elif stage == 1:
            src, dst, to = self.g.at[u, 1 - b2, :, b0], self.r1.at[u], self.p2
        elif stage == 2 and self.kind == "a":
            src, dst, to = self.g.at[u, 1 - b2, b1, b0], self.r2.at[u], self.p2
        elif stage == 2:
            src, dst, to = self.g.at[u, b2, 1 - b1, b0], self.r2.at[u], self.p1
        elif stage == 3:
            src, dst, to = self.g.at[u, b2, b1, b0, self.other_rows], self.r3.at[u], self.q0
        elif stage == 4:
            src, dst, to = self.g.at[u, b2, b1, b0, self.rows, self.other_cols], self.r4.at[u], self.q1
        elif stage == 5:
            src = dst = self.f.at[u, self.rows, self.cols]
            to = self.q1
        else:
            src = dst = self.f.at[u, self.rows]
            to = self.q0
        return pltpu.make_async_remote_copy(
            src, dst, self.send.at[self.index, stage], self.recv.at[self.index, stage],
            device_id=to, device_id_type=MESH,
        )

    def start(self):
        self.copy(0).start()

    def take(self):
        stage = self.stage
        b0, b1, b2 = self.b0, self.b1, self.b2
        self.landed(stage)
        if stage == 0:

            @pl.loop(0, self.count * 4)
            def _(i):
                u, y, x = self.first + lax.div(i, 4), lax.rem(lax.div(i, 2), 2), lax.rem(i, 2)
                add_into(self.g.at[u, y, x, b0], self.r0.at[u, y, x])

        elif stage == 1:

            @pl.loop(0, self.count * 2)
            def _(i):
                u, j = self.first + lax.div(i, 2), lax.rem(i, 2)
                dst = self.g.at[u, j, b1, b0] if self.kind == "a" else self.g.at[u, b2, j, b0]
                add_into(dst, self.r1.at[u, j])

        elif stage <= 4:

            @pl.loop(0, self.count)
            def _(i):
                u = self.first + i
                own = self.g.at[u, b2, b1, b0]
                if stage == 2:
                    add_into(own, self.r2.at[u])
                elif stage == 3:
                    add_into(own.at[self.rows], self.r3.at[u])
                else:
                    mine = own.at[self.rows, self.cols][...].astype(F32)
                    self.f.at[u, self.rows, self.cols][...] = (mine + self.r4[u].astype(F32)).astype(BF)

        self.stage += 1
        if self.stage < self.STAGES:
            self.copy(self.stage).start()

    def landed(self, stage):
        if stage < 5:
            self.copy(stage).wait_recv()
            return
        u = pl.ds(self.first, self.count)
        if stage == 5:
            dst = self.f.at[u, self.rows, self.other_cols]
        else:
            dst = self.f.at[u, self.other_rows]
        pltpu.make_async_copy(dst, dst, self.recv.at[self.index, stage]).wait()

    def close(self):
        for stage in range(self.STAGES):
            self.copy(stage).wait_send()


GROUPS = ((0, 2, "a"), (2, 2, "a"), (4, 2, "b"), (6, 2, "b"), (8, 1, "a"), (9, 1, "b"), (10, 1, "a"), (11, 1, "b"))
UNITS = 12
PLAN = ((0, 2), (1, 3, 4), (0, 2), (1, 3, 4, 0, 2), (5, 0, 2), (1, 3, 4, 0, 2))
HEAD_ROWS = 16


def backward_kernel(
    bits, part_shape,
    ts, buckets, lout, s_in, low1_in, q_in, kv_in, ls_in, do_in, dt_in, gm_in, g_in, wm, small, gains,
    lhome, ihome, f_out, total_out,
    sv, low1, low1t, q2, kv, ls, do, dt, gm, wmv, dkvs, dkvr, dqa, own, dqkv, igv,
    g, r0, r1, r2, r3, r4, f, sm, sr,
    lsend, lrecv, isend, irecv, ksend, krecv, rsend, rrecv, ssend, srecv, wsem, osem,
):
    d, z, c, k = place()
    toks, width = sv.shape
    part = toks // 2
    outer = (1 << len(bits)) // 8
    load = lambda i, src, dst: pltpu.make_async_copy(src, dst, wsem.at[i])
    loads = (
        (g_in, g.at[pl.ds(0, 9)]), (q_in, q2), (kv_in, kv), (do_in, do), (ls_in, ls), (dt_in, dt),
        (low1_in, low1), (wm, wmv), (s_in, sv), (gm_in, gm),
    )
    for i, (src, dst) in enumerate(loads):
        load(i, src, dst).start()
    peers = column_peers() + [(flip(d, bit), z) for bit in bits if bit > 1]
    greet(peers)
    partner = flip(d, 1)
    l_at = lambda i: lout.at[pl.ds(i * part, part)]
    i_at = lambda i: igv.at[pl.ds(i * part, part)]
    swap_start(l_at, lambda s: lhome.at[s], lsend, lrecv)

    refs = (g, r0, r1, r2, r3, r4, f, rsend, rrecv)
    groups = [Reduction(i, *spec, refs, outer) for i, spec in enumerate(GROUPS)]
    load(0, *loads[0]).wait()
    for one in groups[:5]:
        one.start()
    for i in range(1, 7):
        load(i, *loads[i]).wait()
    low1t[...] = low1[...].T

    low_half = iota((1, PAIR), 1) < HEAD_SIZE
    high_half = jnp.logical_not(low_half)
    blk = 256

    def dkv_copy(p):
        return pltpu.make_async_remote_copy(
            dkvs.at[p], dkvr.at[p], ksend.at[p], krecv.at[p], device_id=(partner, z), device_id_type=MESH
        )

    def attend(p, base, store):
        @pl.loop(0, toks // blk)
        def _(b):
            rows = pl.ds(pl.multiple_of(base + b * blk, blk), blk)
            keys, vals = kv[p, 0, rows, :], kv[p, 1, rows, :]
            cols = pl.ds(pl.multiple_of(p * PAIR, PAIR), PAIR)
            q, dout = q2[p], do[:, cols]
            dks, dvs, dq = [], [], None
            for h in range(2):
                half = low_half if h == 0 else high_half
                kh = jnp.where(half, keys, jnp.zeros_like(keys))
                vh = jnp.where(half, vals, jnp.zeros_like(vals))
                probs = jnp.exp(mm_nt(kh, q) - ls[pl.ds(2 * p + h, 1), :])
                ds = (probs * (mm_nt(vh, dout) - dt[pl.ds(2 * p + h, 1), :])).astype(BF)
                dvs.append(mm(probs.astype(BF), dout))
                dks.append(mm(ds, q))
                one = mm_tn(ds, kh)
                dq = one if dq is None else dq + one
            dqa[...] += dq
            store(pl.ds(pl.multiple_of(b * blk, blk), blk),
                  jnp.where(low_half, dks[0], dks[1]), jnp.where(low_half, dvs[0], dvs[1]))

    @pl.loop(0, PAIRS)
    def _(p):
        dqa[...] = jnp.zeros_like(dqa)

        def store_other(rows, dk, dv):
            dkvs[p, 0, rows, :] = dk.astype(BF)
            dkvs[p, 1, rows, :] = dv.astype(BF)

        def store_own(rows, dk, dv):
            own[0, rows, :] = dk
            own[1, rows, :] = dv

        attend(p, (1 - c) * toks, store_other)
        dkv_copy(p).start()
        attend(p, c * toks, store_own)
        dkv_copy(p).wait_recv()
        dq = dqa[...] * 0.125
        dk = pltpu.roll(own[0] + dkvr[p, 0].astype(F32), HEAD_SIZE, 1)
        dv = own[1] + dkvr[p, 1].astype(F32)
        first = pl.multiple_of(p * 3 * PAIR, PAIR)
        dqkv[:, pl.ds(first, PAIR)] = jnp.where(low_half, dq, dk).astype(BF)
        dqkv[:, pl.ds(first + PAIR, PAIR)] = jnp.where(low_half, dv, dq).astype(BF)
        dqkv[:, pl.ds(first + 2 * PAIR, PAIR)] = jnp.where(low_half, dk, dv).astype(BF)

        for i in range(PAIRS):

            @pl.when(p == i)
            def _():
                for one in PLAN[i]:
                    groups[one].take()
                if i % 2 == 1:
                    b = i // 2
                    for h in range(2):
                        res = mm(
                            low1t[h * width // 2 : (h + 1) * width // 2, :],
                            dqkv[:, b * width : (b + 1) * width],
                        ).astype(BF)
                        n = g.shape[-2]
                        for j in range(4):
                            g[9 + b, h, j // 2, j % 2] = res[j * n : (j + 1) * n]
                    groups[5 + b].start()

    for i in range(7, 10):
        load(i, *loads[i]).wait()

    gain0 = gains[0:1, :].astype(F32)
    rows_total = sm.shape[1]
    sm[0, 0:HEAD_ROWS, :] = small[...]
    sums = rows_total - HEAD_ROWS
    here = 4 * k + z
    lanes = iota((1, width), 1)
    scratch = []

    @pl.loop(0, toks // blk)
    def _(b):
        rows = pl.ds(pl.multiple_of(b * blk, blk), blk)
        raw = mm_nt(dqkv[rows, :], wmv[...])
        v = sv[rows, :]
        cen = v - jnp.mean(v, axis=-1, keepdims=True)
        inv = lax.rsqrt(jnp.mean(cen * cen, axis=-1, keepdims=True) + EPS)
        unit = cen * inv
        gr = raw * gain0
        centred = (
            gr - jnp.mean(gr, axis=-1, keepdims=True)
            - unit * jnp.mean(gr * unit, axis=-1, keepdims=True)
        )
        grad = gm[rows, :] + centred * inv
        igv[rows, :] = grad.astype(BF)
        sm[0, 11:12, :] += jnp.sum(raw * unit, axis=0, keepdims=True)
        sm[0, 12:13, :] += jnp.sum(raw, axis=0, keepdims=True)
        sm[0, 13:14, :] += jnp.sum(grad, axis=0, keepdims=True)

    swap_start(i_at, lambda s: ihome.at[s], isend, irecv)
    square = jnp.sum(small[8:9, :]) * (1.0 / (2 * toks * width))
    sm[0, 8:9, :] = jnp.where(lanes == here, square, 0.0)
    first_chip = z == 0
    for row, source in ((9, ts), (10, buckets)):
        a, b = source[0].astype(F32), source[1].astype(F32)
        line = jnp.where(lanes == 2 * d, a, jnp.where(lanes == 2 * d + 1, b, 0.0))
        sm[0, row : row + 1, :] = jnp.where(first_chip, line, jnp.zeros_like(line))
    sm[0, HEAD_ROWS:, :] = jnp.where(iota((sums, 1), 0) == here, sm[0, 13:14, :], 0.0)
    sm[0, 13:14, :] = jnp.zeros((1, width), F32)

    stages = [(flip(d, bit), z) for bit in bits] + [(d, flip(z, 1)), (d, flip(z, 2))]

    def sum_copy(i):
        return pltpu.make_async_remote_copy(
            sm.at[i], sr.at[i], ssend.at[i], srecv.at[i], device_id=stages[i], device_id_type=MESH
        )

    def sum_step(i):
        sum_copy(i).wait_recv()
        sm[i + 1] = sm[i] + sr[i]
        if i + 1 < len(stages):
            sum_copy(i + 1).start()

    sum_copy(0).start()
    waiting = len(stages)
    done = 0
    while any(one.stage < one.STAGES for one in groups) or done < waiting:
        if done < waiting:
            sum_step(done)
            done += 1
        for one in groups:
            if one.stage < one.STAGES:
                one.take()
                if one.stage == one.STAGES:
                    u = pl.ds(one.first, one.count)
                    pltpu.make_async_copy(f.at[u], f_out.at[u], osem.at[one.index]).start()
    total_out[...] = sm[waiting]

    for one in groups:
        one.close()
        u = pl.ds(one.first, one.count)
        pltpu.make_async_copy(f.at[u], f_out.at[u], osem.at[one.index]).wait()
    for i in range(waiting):
        sum_copy(i).wait_send()

    @pl.loop(0, PAIRS)
    def _(p):
        dkv_copy(p).wait_send()

    for s in range(2):
        swap_wait(lambda s: lhome.at[s], lrecv, s)
        swap_wait(lambda s: ihome.at[s], irecv, s)
    swap_sent(l_at, lambda s: lhome.at[s], lsend, lrecv)
    swap_sent(i_at, lambda s: ihome.at[s], isend, irecv)


def run_backward(kept, ts, buckets, wm, gains, dp):
    toks, width = kept["s"].shape
    part = toks // 2
    shard = width // 8
    bits = axis_bits(dp)
    rows = HEAD_ROWS + 2 * dp
    stages = len(bits) + 2
    vm = lambda shape, dtype: pltpu.VMEM(shape, dtype)
    any_ = pl.BlockSpec(memory_space=pl.ANY)
    vmem = pl.BlockSpec(memory_space=pltpu.VMEM)
    smem = pl.BlockSpec(memory_space=pltpu.SMEM)
    dma = lambda *n: pltpu.SemaphoreType.DMA(n)
    count = len(GROUPS)
    return pl.pallas_call(
        functools.partial(backward_kernel, bits, part),
        out_shape=(
            sds((2, part, width), BF), sds((2, part, width), BF), sds((UNITS, shard, width), BF),
            sds((rows, width), F32),
        ),
        in_specs=[smem] * 2 + [any_] * 11 + [vmem] * 2,
        out_specs=(any_, any_, any_, vmem),
        scratch_shapes=[
            vm((toks, width), F32), vm((toks, width), BF), vm((width, toks), BF), vm((PAIRS, toks, PAIR), BF),
            vm((PAIRS, 2, 2 * toks, PAIR), BF), vm((PAIR, toks), F32), vm((toks, width), BF),
            vm((PAIR, toks), F32), vm((toks, width), F32), vm(wm.shape, BF), vm((PAIRS, 2, toks, PAIR), BF),
            vm((PAIRS, 2, toks, PAIR), BF), vm((toks, PAIR), F32), vm((2, toks, PAIR), F32),
            vm((toks, 3 * width), BF), vm((toks, width), BF),
            vm((UNITS, 2, 2, 2, shard, width), BF), vm((UNITS, 2, 2, shard, width), BF),
            vm((UNITS, 2, shard, width), BF), vm((UNITS, shard, width), BF),
            vm((UNITS, shard // 2, width), BF), vm((UNITS, shard // 2, width // 2), BF),
            vm((UNITS, shard, width), BF), vm((stages + 1, rows, width), F32), vm((stages, rows, width), F32),
            dma(2), dma(2), dma(2), dma(2), dma(PAIRS), dma(PAIRS), dma(count, 7), dma(count, 7),
            dma(stages), dma(stages), dma(10), dma(count),
        ],
        compiler_params=pltpu.CompilerParams(
            collective_id=1, has_side_effects=True, vmem_limit_bytes=60 << 20
        ),
        cost_estimate=pl.CostEstimate(flops=16_000_000_000, bytes_accessed=50_000_000, transcendentals=10_000_000),
        name="backward",
    )(
        ts, buckets, kept["lout"], kept["s"], kept["low1"], kept["q"], kept["kv"], kept["ls"], kept["do"],
        kept["dt"], kept["gm"], kept["g"], wm, kept["small"], gains,
    )


def body(
    inputs, cotangent, time_table, timesteps, buckets, mixer_weight, output_weight, up_weight, down_weight,
    norm_gain, norm_shift, output_bias, up_bias,
):
    seqs, part, width = inputs.shape
    dp = lax.axis_size("dp")
    kept = run_forward(
        timesteps, inputs, cotangent, time_table, mixer_weight, output_weight, up_weight, down_weight,
        norm_gain, norm_shift, output_bias, up_bias,
    )
    lhome, ihome, shares, total = run_backward(kept, timesteps, buckets, mixer_weight, norm_gain, dp)
    shares = shares.astype(F32)
    down = shares[0:4].reshape(width // 2, width)
    rest = shares[4:UNITS]
    inner = dp // 8
    if inner > 1:
        teams = [[h * inner + i for i in range(inner)] for h in range(8)]
        scatter = lambda a, axis: lax.psum_scatter(
            a, "dp", scatter_dimension=axis, axis_index_groups=teams, tiled=True
        )
        down, rest = scatter(down, 0), scatter(rest, 1)
    join = lambda a: jnp.concatenate(list(a), axis=-1)
    count = 2 * dp
    columns = width // dp
    steps, places = total[9, :count], total[10, :count]
    sums = lax.dynamic_slice_in_dim(total[HEAD_ROWS:], lax.axis_index("dp") * columns, columns, 1)
    step_hits = (jnp.arange(STEPS, dtype=F32)[:, None] == steps[None, :]).astype(F32)
    table_grad = lax.dot_general(
        step_hits, sums, (((1,), (0,)), ((), ())), precision=lax.Precision.HIGHEST, preferred_element_type=F32
    )
    hits = (jnp.arange(BUCKETS, dtype=F32)[:, None] == places[None, :]).astype(F32)
    return (
        lhome, ihome.astype(F32), join(rest[5:8]), rest[4], join(rest[0:4]), down,
        jnp.stack([total[11], total[0]]), jnp.stack([total[12], total[1]]), total[2:4],
        total[4:8].reshape(-1), table_grad, jnp.sum(hits * total[8:9, :count], axis=1), jnp.sum(hits, axis=1),
    )


def solution(mesh):
    tokens = P("dp", "seq", None)
    return jax.shard_map(
        body,
        mesh=mesh,
        in_specs=(tokens, tokens, P(), P("dp"), P("dp")) + (P(),) * 8,
        out_specs=(tokens, tokens) + (P("dp", None),) * 4 + (P(),) * 4 + (P(None, "dp"), P(), P()),
        check_vma=False,
    )
```

```python
import functools
import math

import jax
import jax.numpy as jnp
from jax import lax
from jax.experimental import pallas as pl
from jax.experimental.pallas import tpu as pltpu
from jax.sharding import PartitionSpec as P

HEADS = 12
HEAD_SIZE = 64
PAIRS = HEADS // 2
PAIR = 2 * HEAD_SIZE
STEPS = 2000
BUCKETS = 8
EPS = 1e-05

BF = jnp.bfloat16
F32 = jnp.float32
MESH = pl.DeviceIdType.MESH


def mm(a, b):
    return lax.dot_general(a, b, (((1,), (0,)), ((), ())), preferred_element_type=F32)


def mm_nt(a, b):
    return lax.dot_general(a, b, (((1,), (1,)), ((), ())), preferred_element_type=F32)


def mm_tn(a, b):
    return lax.dot_general(a, b, (((0,), (0,)), ((), ())), preferred_element_type=F32)


def iota(shape, axis):
    return lax.broadcasted_iota(jnp.int32, shape, axis)


def place():
    d, z = lax.axis_index("dp"), lax.axis_index("seq")
    return d, z, lax.rem(d, 2), lax.div(d, 2)


def column_peers():
    d, z, c, k = place()
    found = []
    for off in range(1, 8):
        m = lax.rem(c * 4 + z + off, 8)
        found.append((2 * k + lax.div(m, 4), lax.rem(m, 4)))
    return found


def greet(ids):
    barrier = pltpu.get_barrier_semaphore()
    for one in ids:
        pl.semaphore_signal(barrier, inc=1, device_id=one, device_id_type=MESH)
    pl.semaphore_wait(barrier, len(ids))


def swap_part(i):
    d, z, c, k = place()
    core, chip = lax.div(z, 2), 2 * c + i
    return core, chip, jnp.logical_and(core == c, chip == z), 2 * k + core


def swap_one(i, source, target, send, recv):
    slot = lax.rem(lax.axis_index("seq"), 2)
    core, chip, own, there = swap_part(i)

    @pl.when(own)
    def _():
        pltpu.make_async_copy(source(i), target(slot), recv.at[slot]).start()

    @pl.when(jnp.logical_not(own))
    def _():
        pltpu.make_async_remote_copy(
            source(i), target(slot), send.at[i], recv.at[slot],
            device_id=(there, chip), device_id_type=MESH,
        ).start()


def swap_start(source, target, send, recv):
    for i in range(2):
        swap_one(i, source, target, send, recv)


def swap_wait(target, recv, s):
    pltpu.make_async_copy(target(s), target(s), recv.at[s]).wait()


def swap_sent(source, target, send, recv):
    for i in range(2):
        core, chip, own, there = swap_part(i)

        @pl.when(jnp.logical_not(own))
        def _():
            pltpu.make_async_remote_copy(
                source(i), target(i), send.at[i], recv.at[i],
                device_id=(there, chip), device_id_type=MESH,
            ).wait_send()


def at(i, n):
    return pl.ds(pl.multiple_of(i * n, n), n)


def flip(index, bit):
    return index + bit - 2 * bit * lax.rem(lax.div(index, bit), 2)


def bit_of(index, bit):
    return lax.rem(lax.div(index, bit), 2)


def axis_bits(size):
    found, bit = [], 1
    while bit < size:
        found.append(bit)
        bit *= 2
    return found


def add_into(dst, *parts):
    total = dst[...].astype(F32)
    for one in parts:
        total = total + one[...].astype(F32)
    dst[...] = total.astype(dst.dtype)


class Reduction:
    def __init__(self, index, kind, g, refs, outer):
        self.index, self.kind, self.g = index, kind, g
        r1, r2, r3, r4, r5, out, self.send, self.recv = refs
        self.out = out.at[index]
        r1, r2, r3, r4, r5 = (r.at[index] for r in (r1, r2, r3, r4, r5))
        d, z, _, _ = place()
        b0, b1, b2 = bit_of(d, outer), bit_of(d, 2 * outer), bit_of(d, 4 * outer)
        near, over_x, over_y = (flip(d, outer), z), (flip(d, 2 * outer), z), (flip(d, 4 * outer), z)
        across = (flip(flip(d, 2 * outer), 4 * outer), z)
        rows, cols = g.shape[-2] // 2, g.shape[-1] // 2
        own = g.at[b2, b1, b0]
        self.used, self.stages = 0, []

        def quarter(ref, q):
            return ref.at[at(lax.rem(q, 2), rows), at(lax.div(q, 2), cols)]

        self.step([(g.at[:, :, 1 - b0], r1, near)], [r1], lambda: self.fold(g, r1, b0))
        if kind[0] == "d":
            moves = [(g.at[b2, 1 - b1, b0], r2.at[0], over_x), (g.at[1 - b2, b1, b0], r2.at[1], over_y),
                     (g.at[1 - b2, 1 - b1, b0], r3, across)]
            self.step(moves, [m[1] for m in moves], lambda: add_into(own, r2.at[0], r2.at[1], r3))
        elif kind[0] == "x":
            self.step([(g.at[:, 1 - b1, b0], r2, over_x)], [r2], lambda: self.fold_x(g, r2, b1, b0))
            self.step([(g.at[1 - b2, b1, b0], r3, over_y)], [r3], lambda: add_into(own, r3))
        else:
            self.step([(g.at[1 - b2, :, b0], r2, over_y)], [r2], lambda: self.fold_y(g, r2, b2, b0))
            self.step([(g.at[b2, 1 - b1, b0], r3, over_x)], [r3], lambda: add_into(own, r3))
        if kind[1] == "s":
            slots = [r4.at[:, pl.ds(0, cols)], r4.at[:, pl.ds(cols, cols)], r5]
            there = [lax.rem(z + o, 4) for o in (1, 2, 3)]
            back = [lax.rem(z + 4 - o, 4) for o in (1, 2, 3)]
            moves = [(quarter(own, there[i]), slots[i], (d, there[i])) for i in range(3)]
            self.step(moves, slots, lambda: self.finish(quarter(own, z), quarter(self.out, z), slots))
            mine = quarter(self.out, z)
            self.step([(mine, mine, (d, one)) for one in there], [quarter(self.out, one) for one in back], None)
        else:
            z0, z1 = lax.rem(z, 2), lax.div(z, 2)
            mine, other = at(z0, rows), at(1 - z0, rows)
            left, right = at(z1, cols), at(1 - z1, cols)
            half = own.at[mine]
            one, two = (d, flip(z, 1)), (d, flip(z, 2))
            self.step([(own.at[other], r4, one)], [r4], lambda: add_into(half, r4))
            self.step(
                [(own.at[mine, right], r5, two)], [r5],
                lambda: self.finish(own.at[mine, left], self.out.at[mine, left], [r5]),
            )
            done = self.out.at[mine, left]
            self.step([(done, done, two)], [self.out.at[mine, right]], None)
            done = self.out.at[mine]
            self.step([(done, done, one)], [self.out.at[other]], None)

    def step(self, moves, landing, combine):
        first = self.used
        self.used += len(moves)
        copies = [
            pltpu.make_async_remote_copy(
                src, dst, self.send.at[self.index, first + i], self.recv.at[self.index, first + i],
                device_id=to, device_id_type=MESH,
            )
            for i, (src, dst, to) in enumerate(moves)
        ]
        waits = [
            pltpu.make_async_copy(here, here, self.recv.at[self.index, first + i])
            for i, here in enumerate(landing)
        ]
        self.stages.append((copies, waits, combine))

    def fold(self, g, r, b0):
        @pl.loop(0, 4)
        def _(i):
            y, x = lax.div(i, 2), lax.rem(i, 2)
            add_into(g.at[y, x, b0], r.at[y, x])

    def fold_x(self, g, r, b1, b0):
        @pl.loop(0, 2)
        def _(i):
            add_into(g.at[i, b1, b0], r.at[i])

    def fold_y(self, g, r, b2, b0):
        @pl.loop(0, 2)
        def _(i):
            add_into(g.at[b2, i, b0], r.at[i])

    def finish(self, own, out, parts):
        total = own[...].astype(F32)
        for one in parts:
            total = total + one[...].astype(F32)
        out[...] = total.astype(out.dtype)

    def start(self):
        for copy in self.stages[0][0]:
            copy.start()

    def take(self, stage):
        _, waits, combine = self.stages[stage]
        for one in waits:
            one.wait()
        if combine is not None:
            combine()
        if stage + 1 < len(self.stages):
            for copy in self.stages[stage + 1][0]:
                copy.start()

    def ends(self, stage):
        return stage + 1 == len(self.stages)

    def close(self):
        for copies, _, _ in self.stages:
            for copy in copies:
                copy.wait_send()


KINDS = ("xs", "ys", "xs", "yh", "xh", "yh", "xh", "yh", "dh", "dh", "dh", "xs")
EARLY = 9
UNITS = 12
VECTORS, LOUT, GRAD = 12, 13, 15
SCHEDULE = (
    ((13, 0), (14, 0), (0, 0)),
    ((1, 0),),
    (),
    (),
    ((2, 0),),
    ((3, 0),),
    (),
    ((1, 1),),
    ((5, 0),),
    ((4, 0),),
    ((2, 1), (1, 2)),
    ((5, 1), (7, 0), (1, 3)),
    ((3, 2), (0, 2)),
    ((2, 3), (3, 3), (7, 1)),
    ((2, 4), (7, 2)),
    (),
    ((3, 1), (0, 1)),
    ((2, 2), (6, 0)),
    ((1, 4), (4, 1), (5, 2)),
    ((5, 3), (6, 1), (4, 2), (0, 3), (8, 0)),
    ((3, 4), (4, 3), (5, 4), (6, 2)),
    ((15, 0), (3, 5), (0, 4), (7, 3), (10, 0)),
)
TAIL = (
    (16, 0), (9, 0), (4, 4), (11, 0), (6, 3), (8, 1), (5, 5), (12, 0), (3, 6), (10, 1),
    (7, 4), (9, 1), (8, 2), (11, 1), (5, 6), (12, 1), (4, 5), (10, 2), (6, 4), (9, 2),
    (7, 5), (11, 2), (8, 3), (4, 6), (12, 2), (10, 3), (6, 5), (7, 6), (9, 3), (11, 3),
    (8, 4), (12, 3), (10, 4), (6, 6), (9, 4), (11, 4), (8, 5), (12, 4), (10, 5), (9, 5),
)
HEAD_ROWS = 16
STEP = 768


def sds(shape, dtype):
    return jax.ShapeDtypeStruct(shape, dtype)


def norm_parts(v):
    cen = v - jnp.mean(v, axis=-1, keepdims=True)
    inv = lax.rsqrt(jnp.mean(cen * cen, axis=-1, keepdims=True) + EPS)
    return cen * inv, inv


def norm_back(raw, unit, inv, gain):
    g = raw * gain
    return inv * (
        g - jnp.mean(g, axis=-1, keepdims=True) - unit * jnp.mean(g * unit, axis=-1, keepdims=True)
    )


class Return:
    def __init__(self, i, *refs):
        self.i, self.refs = i, refs

    def take(self, stage):
        swap_one(self.i, *self.refs)


class VectorSum:
    def __init__(self, sm, sr, send, recv, partners):
        self.sm, self.sr = sm, sr
        self.copies = [
            pltpu.make_async_remote_copy(
                sm.at[i % 2], sr.at[i], send.at[i], recv.at[i], device_id=to, device_id_type=MESH
            )
            for i, to in enumerate(partners)
        ]

    def start(self):
        self.copies[0].start()

    def take(self, i):
        self.copies[i].wait_recv()
        if i:
            self.copies[i - 1].wait_send()
        self.sm[(i + 1) % 2] = self.sm[i % 2] + self.sr[i]
        if i + 1 < len(self.copies):
            self.copies[i + 1].start()

    def close(self):
        self.copies[-1].wait_send()


def layer_kernel(
    bits,
    ts, buckets, x, cot, table, wm, wo, wu, wd, gains, shifts, biases, upb,
    lhome, ihome, f_out, total_out,
    xr, cr, embs, embr, kv, dkvr, r1, r2, r3, r4, r5, f, sm, sr,
    low1, q2, mixed, do, gm, lov, g, ls, lst, dt, upg,
    xsend, xrecv, csend, crecv, esend, erecv, ksend, krecv, lsend, lrecv, isend, irecv,
    dsend, drecv, rsend, rrecv, ssend, srecv, wsem, osem,
):
    d, z, c, k = place()
    toks, width = xr.shape
    part = toks // 2
    ff = wu.shape[1]
    blk = toks // 2
    outer = (1 << len(bits)) // 8
    partner = flip(d, 1)
    row_of = lambda ref, i: ref[i : i + 1, :].astype(F32)
    load = lambda i, src, dst: pltpu.make_async_copy(src, dst, wsem.at[i])
    x_at, c_at = lambda s: xr.at[at(s, part)], lambda s: cr.at[at(s, part)]
    l_at = lambda s: lov.at[at(s, part)]
    low_half = iota((1, PAIR), 1) < HEAD_SIZE
    high_half = jnp.logical_not(low_half)
    lane = iota((1, PAIR), 1)
    mine = at(c, toks)

    across = (flip(flip(d, 2 * outer), 4 * outer), z)
    greet(column_peers() + [(flip(d, bit), z) for bit in bits if bit > 1] + [across])
    swap_start(lambda i: x.at[i], x_at, xsend, xrecv)
    refs = (r1, r2, r3, r4, r5, f, rsend, rrecv)
    units = {i: Reduction(i, KINDS[i], g.at[i], refs, outer) for i in range(EARLY)}
    for i in range(2):
        units[LOUT + i] = Return(i, l_at, lambda s: lhome.at[s], lsend, lrecv)
    plan = iter(SCHEDULE)

    def point():
        for one, stage in next(plan):
            units[one].take(stage)

    def points(count, index):
        for i, row in enumerate([next(plan) for _ in range(count)]):
            if row:

                @pl.when(index == i)
                def _():
                    for one, stage in row:
                        units[one].take(stage)

    def kv_copy(p):
        return pltpu.make_async_remote_copy(
            kv.at[p, :, mine], kv.at[p, :, mine], ksend.at[p], krecv.at[p],
            device_id=(partner, z), device_id_type=MESH,
        )

    def project(wmv, tabv):
        load(1, wm, wmv).start()
        load(0, table, tabv).start()
        load(0, table, tabv).wait()
        row, col = iota((16, tabv.shape[0]), 0), iota((16, tabv.shape[0]), 1)
        wanted = jnp.where(row == 0, ts[0], ts[1])
        hits = jnp.where(jnp.logical_and(col == wanted, row < 2), 1.0, 0.0).astype(BF)
        picked = mm(hits, tabv[...])
        for i in range(2):
            embs[i] = jnp.broadcast_to(picked[i : i + 1], (16, width)).astype(BF)
        swap_start(lambda i: embs.at[i], lambda s: embr.at[s], esend, erecv)
        for s in range(2):
            swap_wait(lambda s: embr.at[s], erecv, s)
        gain, shift = row_of(gains, 0), row_of(shifts, 0)
        for s in range(2):
            swap_wait(x_at, xrecv, s)
            emb = embr[s][0:1, :].astype(F32)

            @pl.loop(0, part // 128)
            def _(b):
                rows = pl.ds(pl.multiple_of(s * part + b * 128, 128), 128)
                unit, _ = norm_parts(xr[rows, :].astype(F32) + emb)
                low1[rows, :] = (unit * gain + shift).astype(BF)

        swap_start(lambda i: cot.at[i], c_at, csend, crecv)
        load(1, wm, wmv).wait()

        @pl.loop(0, PAIRS // 2)
        def _(i):
            res = mm(low1[...], wmv[:, at(i, 6 * PAIR)])
            for j in range(2):
                p = 2 * i + j
                t0, t1, t2 = (res[:, (3 * j + n) * PAIR : (3 * j + n + 1) * PAIR] for n in range(3))
                q2[p] = (jnp.where(low_half, t0, t1).astype(BF) * 0.125).astype(BF)
                kv[p, 0, mine, :] = pltpu.roll(jnp.where(low_half, t2, t0), HEAD_SIZE, 1).astype(BF)
                kv[p, 1, mine, :] = jnp.where(low_half, t1, t2).astype(BF)
                kv_copy(p).start()

    def attend():
        @pl.loop(0, PAIRS)
        def _(p):
            kv_copy(p).wait_recv()
            q, keys, vals = q2[p], kv[p, 0], kv[p, 1]
            scores = [mm_nt(jnp.where(half, q, jnp.zeros_like(q)), keys) for half in (low_half, high_half)]
            tops = [jnp.max(s, axis=-1, keepdims=True) for s in scores]
            powers = [jnp.exp(s - top) for s, top in zip(scores, tops)]
            lows = [e.astype(BF) for e in powers]
            totals = [jnp.sum(e, axis=-1, keepdims=True) for e in powers]
            outs = [mm(e, vals) * (1.0 / total) for e, total in zip(lows, totals)]
            sums = [top + jnp.log(total) for top, total in zip(tops, totals)]
            mixed[:, at(p, PAIR)] = jnp.where(low_half, *outs).astype(BF)
            ls[...] = jnp.where(lane == 2 * p, sums[0], jnp.where(lane == 2 * p + 1, sums[1], ls[...]))

        lst[...] = ls[...].T

    def feed(wov, wuv, wdv, mid, low2, low2t, hid, rl):
        load(2, wo, wov).wait()
        gain, shift, bias = row_of(gains, 1), row_of(shifts, 1), row_of(biases, 0)

        @pl.loop(0, 2)
        def _(b):
            rows = at(b, blk)
            v = xr[rows, :].astype(F32) + embr[b][0:1, :].astype(F32)
            v = v + mm(mixed[rows, :], wov[...]) + bias
            mid[rows, :] = v
            low2[rows, :] = (norm_parts(v)[0] * gain + shift).astype(BF)

        low2t[...] = low2[...].T
        load(3, wu, wuv).wait()
        load(4, wd, wdv).wait()
        for s in range(2):
            swap_wait(c_at, crecv, s)

        @pl.loop(0, ff // STEP)
        def _(j):
            cols = at(j, STEP)
            r = mm(low2[...], wuv[:, cols]) + upb[:, cols].astype(F32)
            back = mm_nt(cr[...], wdv[cols, :])
            half = 0.5 * (1.0 + lax.erf(r * math.sqrt(0.5)))
            bell = jnp.exp(r * r * -0.5) * (1.0 / math.sqrt(2.0 * math.pi))
            hid[:, cols] = (r * half).astype(BF)
            low = (back * (half + r * bell)).astype(BF)
            rl[:, cols] = low
            upg[:, cols] = jnp.sum(low.astype(F32), axis=0, keepdims=True)

        n = g.shape[-2]

        @pl.loop(0, 4)
        def _(j):
            res = mm_tn(hid[:, at(j, width)], cr[...]).astype(BF)
            for s in range(2):
                for i in range(4):
                    first = (4 * s + i) * n
                    g[i, lax.div(j, 2), lax.rem(j, 2), s] = res[first : first + n]

        for i in range(4):
            units[i].start()
        fin = mid[...] + mm(hid[...], wdv[...]) + row_of(biases, 1)
        lov[...] = fin.astype(BF)
        sm[0, 8:9, :] = jnp.sum(fin * fin, axis=0, keepdims=True)
        point()

        @pl.loop(0, 4)
        def _(j):
            res = mm(low2t[...], rl[:, at(j, width)]).astype(BF)
            for i in range(8):
                g[4 + j, i // 4, (i // 2) % 2, i % 2] = res[i * n : (i + 1) * n]
            for i in range(4):

                @pl.when(j == i)
                def _():
                    units[4 + i].start()

            points(4, j)

        gm[...] = mm_nt(rl[...], wuv[...])
        point()

        @pl.loop(0, toks // 128)
        def _(b):
            rows = at(b, 128)
            unit, inv = norm_parts(mid[rows, :])
            raw = gm[rows, :]
            ct = cr[rows, :].astype(F32)
            grad = ct + norm_back(raw, unit, inv, gain)
            gm[rows, :] = grad
            sm[0, 0:1, :] += jnp.sum(raw * unit, axis=0, keepdims=True)
            sm[0, 1:2, :] += jnp.sum(raw, axis=0, keepdims=True)
            sm[0, 2:3, :] += jnp.sum(grad.astype(BF).astype(F32), axis=0, keepdims=True)
            sm[0, 3:4, :] += jnp.sum(ct, axis=0, keepdims=True)

        for i in range(4):
            sm[0, 4 + i : 5 + i, :] = upg[:, i * width : (i + 1) * width]
        point()
        res = mm_tn(mixed[...], gm[...].astype(BF)).astype(BF)
        for i in range(8):
            g[8, i // 4, (i // 2) % 2, i % 2] = res[i * n : (i + 1) * n]
        units[8].start()
        point()
        fold = lax.div(iota((PAIR, width), 1), HEAD_SIZE) == iota((PAIR, width), 0)
        fold = jnp.where(fold, 1.0, 0.0).astype(BF)
        dout = mm_nt(gm[...].astype(BF), wov[...]).astype(BF)
        do[...] = dout
        prod = dout.astype(F32) * mixed[...].astype(F32)
        high = prod.astype(BF)
        rest = (prod - high.astype(F32)).astype(BF)
        dt[...] = mm_nt(fold, high) + mm_nt(fold, rest)
        point()

    def forward(wov, wuv, wdv):
        load(2, wo, wov).start()
        load(3, wu, wuv).start()
        load(4, wd, wdv).start()
        sm[0] = jnp.zeros_like(sm[0])
        pl.run_scoped(project, pltpu.VMEM(wm.shape, BF), pltpu.VMEM(table.shape, BF))
        attend()
        pl.run_scoped(
            functools.partial(feed, wov, wuv, wdv),
            pltpu.VMEM((toks, width), F32), pltpu.VMEM((toks, width), BF), pltpu.VMEM((width, toks), BF),
            pltpu.VMEM((toks, ff), BF), pltpu.VMEM((toks, ff), BF),
        )

    pl.run_scoped(forward, pltpu.VMEM(wo.shape, BF), pltpu.VMEM(wu.shape, BF), pltpu.VMEM(wd.shape, BF))

    def backward(wmv, low1t, late_g, dkvs, dqa, dqkv, igv):
        load(5, wm, wmv).start()
        low1t[...] = low1[...].T
        for i in range(EARLY, UNITS):
            units[i] = Reduction(i, KINDS[i], late_g.at[i - EARLY], refs, outer)
        i_at = lambda s: igv.at[at(s, part)]

        def dkv_copy(p):
            return pltpu.make_async_remote_copy(
                dkvs.at[p], dkvr.at[p], dsend.at[p], drecv.at[p],
                device_id=(partner, z), device_id_type=MESH,
            )

        halves = (low_half, high_half)

        def attend_back(p, base):
            rows = pl.ds(pl.multiple_of(base, toks), toks)
            keys, vals = kv[p, 0, rows, :], kv[p, 1, rows, :]
            q, dout = q2[p], do[:, at(p, PAIR)]
            dks, dvs, dqs = [], [], []
            for h, half in enumerate(halves):
                kh = jnp.where(half, keys, jnp.zeros_like(keys))
                vh = jnp.where(half, vals, jnp.zeros_like(vals))
                probs = jnp.exp(mm_nt(kh, q) - lst[pl.ds(2 * p + h, 1), :])
                ds = (probs * (mm_nt(vh, dout) - dt[pl.ds(2 * p + h, 1), :])).astype(BF)
                dvs.append(mm(probs.astype(BF), dout))
                dks.append(mm(ds, q))
                dqs.append(mm_tn(ds, kh))
            return jnp.where(low_half, *dks), jnp.where(low_half, *dvs), dqs[0] + dqs[1]

        @pl.loop(0, PAIRS)
        def _(p):
            dk, dv, dq = attend_back(p, (1 - c) * toks)
            dkvs[p, 0] = dk.astype(BF)
            dkvs[p, 1] = dv.astype(BF)
            dqa[...] = dq
            dkv_copy(p).start()
            points(PAIRS, p)
            dk, dv, dq = attend_back(p, c * toks)
            dkv_copy(p).wait_recv()
            dq = (dq + dqa[...]) * 0.125
            dk = pltpu.roll(dk + dkvr[p, 0].astype(F32), HEAD_SIZE, 1)
            dv = dv + dkvr[p, 1].astype(F32)
            dqkv[:, at(3 * p, PAIR)] = jnp.where(low_half, dq, dk).astype(BF)
            dqkv[:, at(3 * p + 1, PAIR)] = jnp.where(low_half, dv, dq).astype(BF)
            dqkv[:, at(3 * p + 2, PAIR)] = jnp.where(low_half, dk, dv).astype(BF)

            @pl.when(lax.rem(p, 2) == 1)
            def _():
                b = lax.div(p, 2)
                n = g.shape[-2]
                res = mm(low1t[...], dqkv[:, at(b, width)]).astype(BF)
                for j in range(8):
                    late_g[b, j // 4, (j // 2) % 2, j % 2] = res[j * n : (j + 1) * n]
                for i in range(3):

                    @pl.when(b == i)
                    def _():
                        units[EARLY + i].start()

            points(PAIRS, p)

        load(5, wm, wmv).wait()
        gain0 = row_of(gains, 0)
        here = 4 * k + z
        lanes = iota((1, width), 1)

        @pl.loop(0, 2)
        def _(b):
            rows = at(b, blk)
            raw = mm_nt(dqkv[rows, :], wmv[...])
            unit, inv = norm_parts(xr[rows, :].astype(F32) + embr[b][0:1, :].astype(F32))
            grad = gm[rows, :] + norm_back(raw, unit, inv, gain0)
            igv[rows, :] = grad.astype(BF)
            sm[0, 11:12, :] += jnp.sum(raw * unit, axis=0, keepdims=True)
            sm[0, 12:13, :] += jnp.sum(raw, axis=0, keepdims=True)
            sm[0, 13:14, :] += jnp.sum(grad, axis=0, keepdims=True)

        square = jnp.sum(sm[0, 8:9, :]) * (1.0 / (2 * toks * width))
        sm[0, 8:9, :] = jnp.where(lanes == here, square, 0.0)
        for row, source in ((9, ts), (10, buckets)):
            first, second = source[0].astype(F32), source[1].astype(F32)
            line = jnp.where(lanes == 2 * d, first, jnp.where(lanes == 2 * d + 1, second, 0.0))
            sm[0, row : row + 1, :] = jnp.where(z == 0, line, jnp.zeros_like(line))
        sums = sm.shape[1] - HEAD_ROWS
        sm[0, HEAD_ROWS:, :] = jnp.where(iota((sums, 1), 0) == here, sm[0, 13:14, :], 0.0)
        stages = [(flip(d, bit), z) for bit in bits] + [(d, flip(z, 1)), (d, flip(z, 2))]

        vectors = VectorSum(sm, sr, ssend, srecv, stages)
        units[VECTORS] = vectors
        for i in range(2):
            units[GRAD + i] = Return(i, i_at, lambda s: ihome.at[s], isend, irecv)
        vectors.start()

        def put(i):
            return pltpu.make_async_copy(f.at[i], f_out.at[i], osem.at[i])

        point()
        for one, stage in TAIL:
            units[one].take(stage)
            if one < UNITS and units[one].ends(stage):
                put(one).start()
        for one in range(UNITS):
            if not any(i == one and units[one].ends(stage) for i, stage in TAIL):
                put(one).start()
        extra = len(stages) - 5
        for i in range(extra):
            vectors.take(5 + i)
        result = pltpu.make_async_copy(sm.at[len(stages) % 2], total_out, wsem.at[0])
        result.start()
        for i in range(UNITS + 1):
            units[i].close()
        for i in range(UNITS):
            put(i).wait()
        result.wait()

        @pl.loop(0, PAIRS)
        def _(p):
            kv_copy(p).wait_send()
            dkv_copy(p).wait_send()

        for s in range(2):
            swap_wait(lambda s: lhome.at[s], lrecv, s)
            swap_wait(lambda s: ihome.at[s], irecv, s)
        swap_sent(lambda i: x.at[i], x_at, xsend, xrecv)
        swap_sent(lambda i: cot.at[i], c_at, csend, crecv)
        swap_sent(lambda i: embs.at[i], lambda s: embr.at[s], esend, erecv)
        swap_sent(l_at, lambda s: lhome.at[s], lsend, lrecv)
        swap_sent(i_at, lambda s: ihome.at[s], isend, irecv)

    shard = g.shape[-2]
    pl.run_scoped(
        backward,
        pltpu.VMEM(wm.shape, BF), pltpu.VMEM((width, toks), BF),
        pltpu.VMEM((UNITS - EARLY, 2, 2, 2, shard, width), BF), pltpu.VMEM((PAIRS, 2, toks, PAIR), BF),
        pltpu.VMEM((toks, PAIR), F32), pltpu.VMEM((toks, 3 * width), BF),
        pltpu.VMEM((toks, width), BF),
    )


def run_layer(ts, buckets, x, cot, table, wm, wo, wu, wd, gains, shifts, biases, upb, dp):
    _, part, width = x.shape
    toks = 2 * part
    ff = wu.shape[1]
    shard = width // 8
    bits = axis_bits(dp)
    rows = HEAD_ROWS + 2 * dp
    stages = len(bits) + 2
    vm = lambda shape, dtype: pltpu.VMEM(shape, dtype)
    any_ = pl.BlockSpec(memory_space=pl.ANY)
    vmem = pl.BlockSpec(memory_space=pltpu.VMEM)
    smem = pl.BlockSpec(memory_space=pltpu.SMEM)
    dma = lambda *n: pltpu.SemaphoreType.DMA(n)
    return pl.pallas_call(
        functools.partial(layer_kernel, bits),
        out_shape=(
            sds((2, part, width), BF), sds((2, part, width), BF), sds((UNITS, shard, width), BF),
            sds((rows, width), F32),
        ),
        in_specs=[smem] * 2 + [any_] * 7 + [vmem] * 4,
        out_specs=(any_,) * 4,
        scratch_shapes=[
            vm((toks, width), BF), vm((toks, width), BF), vm((2, 16, width), BF), vm((2, 16, width), BF),
            vm((PAIRS, 2, 2 * toks, PAIR), BF), vm((PAIRS, 2, toks, PAIR), BF),
            vm((UNITS, 2, 2, shard, width), BF), vm((UNITS, 2, shard, width), BF), vm((UNITS, shard, width), BF),
            vm((UNITS, shard // 2, width), BF), vm((UNITS, shard // 2, width // 2), BF),
            vm((UNITS, shard, width), BF), vm((2, rows, width), F32), vm((stages, rows, width), F32),
            vm((toks, width), BF), vm((PAIRS, toks, PAIR), BF), vm((toks, width), BF), vm((toks, width), BF),
            vm((toks, width), F32), vm((toks, width), BF), vm((EARLY, 2, 2, 2, shard, width), BF),
            vm((toks, PAIR), F32), vm((PAIR, toks), F32), vm((PAIR, toks), F32), vm((1, ff), F32),
            dma(2), dma(2), dma(2), dma(2), dma(2), dma(2), dma(PAIRS), dma(PAIRS),
            dma(2), dma(2), dma(2), dma(2), dma(PAIRS), dma(PAIRS), dma(UNITS, 10), dma(UNITS, 10),
            dma(stages), dma(stages), dma(6), dma(UNITS),
        ],
        compiler_params=pltpu.CompilerParams(
            collective_id=0, has_side_effects=True, vmem_limit_bytes=127 << 19
        ),
        cost_estimate=pl.CostEstimate(
            flops=32_000_000_000, bytes_accessed=60_000_000, transcendentals=20_000_000
        ),
        name="layer",
    )(ts, buckets, x, cot, table, wm, wo, wu, wd, gains, shifts, biases, upb.reshape(1, ff))


def finish_kernel(
    lhome, ihome_in, f_in, total_in, layer_out, input_grad, mixer, output, up, down, gains, shifts, biases, upb,
    table, norms, counts, ihome, f, total, sem,
):
    n, width = f.shape[1:]
    columns, step_count = table.shape
    copies = [
        pltpu.make_async_copy(src, dst, sem.at[i])
        for i, (src, dst) in enumerate(((total_in, total), (f_in, f), (ihome_in, ihome), (lhome, layer_out)))
    ]
    for one in copies:
        one.start()
    copies[0].wait()
    for i in range(4):
        upb[pl.ds(i * width, width)] = total[4 + i, :]
    for i, row in enumerate((11, 0)):
        gains[i : i + 1, :] = total[row : row + 1, :]
        shifts[i : i + 1, :] = total[row + 1 : row + 2, :]
    biases[...] = total[2:4, :]
    count = total.shape[0] - HEAD_ROWS
    first = lax.axis_index("dp") * columns
    chosen = iota((width, columns), 0) == iota((width, columns), 1) + first
    chosen = jnp.where(chosen, 1.0, 0.0).astype(BF)
    steps = total[9:10, :count]
    hits = jnp.where(iota((step_count, count), 0).astype(F32) == steps, 1.0, 0.0).astype(BF)
    here = iota((BUCKETS, count), 0).astype(F32) == total[10:11, :count]
    here = jnp.where(here, 1.0, 0.0).astype(BF)
    rest, grad = total[HEAD_ROWS:, :], 0.0
    means = jnp.where(iota((8, count), 0) == 0, total[8:9, :count], 1.0)
    norm = 0.0
    for _ in range(3):
        piece = rest.astype(BF)
        rest = rest - piece.astype(F32)
        part = mm(piece, chosen).astype(BF)
        grad = grad + lax.dot_general(part, hits, (((0,), (1,)), ((), ())), preferred_element_type=F32)
        piece = means.astype(BF)
        means = means - piece.astype(F32)
        norm = norm + mm_nt(piece, here)
    table[...] = grad
    norms[...] = norm[0, :]
    counts[...] = norm[1, :]
    copies[1].wait()
    for i in range(4):
        down[i * n : (i + 1) * n, :] = f[i].astype(F32)
        up[:, i * width : (i + 1) * width] = f[4 + i].astype(F32)
    output[...] = f[8].astype(F32)
    for i in range(3):
        mixer[:, i * width : (i + 1) * width] = f[9 + i].astype(F32)
    copies[2].wait()
    input_grad[...] = ihome[...].astype(F32)
    copies[3].wait()


def run_finish(lhome, ihome, f, total, dp, steps):
    n, width = f.shape[1:]
    outs = [
        sds(lhome.shape, BF), sds(ihome.shape, F32), sds((n, 3 * width), F32), sds((n, width), F32),
        sds((n, 4 * width), F32), sds((4 * n, width), F32), sds((2, width), F32), sds((2, width), F32),
        sds((2, width), F32), sds((4 * width,), F32), sds((width // dp, steps), F32), sds((BUCKETS,), F32),
        sds((BUCKETS,), F32),
    ]
    vmem, any_ = pl.BlockSpec(memory_space=pltpu.VMEM), pl.BlockSpec(memory_space=pl.ANY)
    res = pl.pallas_call(
        finish_kernel,
        out_shape=outs,
        in_specs=[any_] * 4,
        out_specs=[vmem] * len(outs),
        scratch_shapes=[
            pltpu.VMEM(ihome.shape, BF), pltpu.VMEM(f.shape, f.dtype), pltpu.VMEM(total.shape, F32),
            pltpu.SemaphoreType.DMA((4,)),
        ],
        compiler_params=pltpu.CompilerParams(vmem_limit_bytes=60 << 20),
        name="finish",
    )(lhome, ihome, f, total)
    return (*res[:10], res[10].T, *res[11:])


def body(
    inputs, cotangent, time_table, timesteps, buckets, mixer_weight, output_weight, up_weight, down_weight,
    norm_gain, norm_shift, output_bias, up_bias,
):
    width = inputs.shape[-1]
    dp = lax.axis_size("dp")
    lhome, ihome, shares, total = run_layer(
        timesteps, buckets, inputs, cotangent, time_table, mixer_weight, output_weight, up_weight,
        down_weight, norm_gain, norm_shift, output_bias, up_bias, dp,
    )
    inner = dp // 8
    if inner > 1:
        teams = [[h * inner + i for i in range(inner)] for h in range(8)]
        scatter = lambda a, axis: lax.psum_scatter(
            a, "dp", scatter_dimension=axis, axis_index_groups=teams, tiled=True
        )
        shares = shares.astype(F32)
        down, rest = scatter(shares[0:4].reshape(width // 2, width), 0), scatter(shares[4:UNITS], 1)
        shares = jnp.concatenate([down.reshape((4,) + rest.shape[1:]), rest])
    return run_finish(lhome, ihome, shares, total, dp, time_table.shape[0])


def solution(mesh):
    tokens = P("dp", "seq", None)
    return jax.shard_map(
        body,
        mesh=mesh,
        in_specs=(tokens, tokens, P(), P("dp"), P("dp")) + (P(),) * 8,
        out_specs=(tokens, tokens) + (P("dp", None),) * 4 + (P(),) * 4 + (P(None, "dp"), P(), P()),
        check_vma=False,
    )
```

```python
import functools
import math

import jax
import jax.numpy as jnp
from jax import lax
from jax.experimental import pallas as pl
from jax.experimental.pallas import tpu as pltpu
from jax.sharding import PartitionSpec as P

HEADS = 12
HEAD_SIZE = 64
PAIRS = HEADS // 2
PAIR = 2 * HEAD_SIZE
STEPS = 2000
BUCKETS = 8
EPS = 1e-05

BF = jnp.bfloat16
F32 = jnp.float32
MESH = pl.DeviceIdType.MESH


def mm(a, b):
    return lax.dot_general(a, b, (((1,), (0,)), ((), ())), preferred_element_type=F32)


def mm_nt(a, b):
    return lax.dot_general(a, b, (((1,), (1,)), ((), ())), preferred_element_type=F32)


def mm_tn(a, b):
    return lax.dot_general(a, b, (((0,), (0,)), ((), ())), preferred_element_type=F32)


def iota(shape, axis):
    return lax.broadcasted_iota(jnp.int32, shape, axis)


def place():
    d, z = lax.axis_index("dp"), lax.axis_index("seq")
    return d, z, lax.rem(d, 2), lax.div(d, 2)


def column_peers():
    d, z, c, k = place()
    found = []
    for off in range(1, 8):
        m = lax.rem(c * 4 + z + off, 8)
        found.append((2 * k + lax.div(m, 4), lax.rem(m, 4)))
    return found


def greet(ids):
    barrier = pltpu.get_barrier_semaphore()
    for one in ids:
        pl.semaphore_signal(barrier, inc=1, device_id=one, device_id_type=MESH)
    pl.semaphore_wait(barrier, len(ids))


def swap_part(i):
    d, z, c, k = place()
    core, chip = lax.div(z, 2), 2 * c + i
    return core, chip, jnp.logical_and(core == c, chip == z), 2 * k + core


def swap_one(i, source, target, send, recv):
    slot = lax.rem(lax.axis_index("seq"), 2)
    core, chip, own, there = swap_part(i)

    @pl.when(own)
    def _():
        pltpu.make_async_copy(source(i), target(slot), recv.at[slot]).start()

    @pl.when(jnp.logical_not(own))
    def _():
        pltpu.make_async_remote_copy(
            source(i), target(slot), send.at[i], recv.at[slot],
            device_id=(there, chip), device_id_type=MESH,
        ).start()


def swap_start(source, target, send, recv):
    for i in range(2):
        swap_one(i, source, target, send, recv)


def swap_wait(target, recv, s):
    pltpu.make_async_copy(target(s), target(s), recv.at[s]).wait()


def swap_sent(source, target, send, recv):
    for i in range(2):
        core, chip, own, there = swap_part(i)

        @pl.when(jnp.logical_not(own))
        def _():
            pltpu.make_async_remote_copy(
                source(i), target(i), send.at[i], recv.at[i],
                device_id=(there, chip), device_id_type=MESH,
            ).wait_send()


def at(i, n):
    return pl.ds(pl.multiple_of(i * n, n), n)


def flip(index, bit):
    return index + bit - 2 * bit * lax.rem(lax.div(index, bit), 2)


def bit_of(index, bit):
    return lax.rem(lax.div(index, bit), 2)


def axis_bits(size):
    found, bit = [], 1
    while bit < size:
        found.append(bit)
        bit *= 2
    return found


def add_into(dst, *parts):
    total = dst[...].astype(F32)
    for one in parts:
        total = total + one[...].astype(F32)
    dst[...] = total.astype(dst.dtype)


class Reduction:
    def __init__(self, index, kind, g, refs, outer):
        self.index, self.kind, self.g = index, kind, g
        r1, r2, r3, r4, r5, out, self.send, self.recv = refs
        self.out = out.at[index]
        r1, r2, r3, r4, r5 = (r.at[index] for r in (r1, r2, r3, r4, r5))
        d, z, _, _ = place()
        b0, b1, b2 = bit_of(d, outer), bit_of(d, 2 * outer), bit_of(d, 4 * outer)
        near, over_x, over_y = (flip(d, outer), z), (flip(d, 2 * outer), z), (flip(d, 4 * outer), z)
        across = (flip(flip(d, 2 * outer), 4 * outer), z)
        rows, cols = g.shape[-2] // 2, g.shape[-1] // 2
        own = g.at[b2, b1, b0]
        self.used, self.stages = 0, []

        def quarter(ref, q):
            return ref.at[at(lax.rem(q, 2), rows), at(lax.div(q, 2), cols)]

        self.step([(g.at[:, :, 1 - b0], r1, near)], [r1], lambda: self.fold(g, r1, b0))
        if kind[0] == "d":
            moves = [(g.at[b2, 1 - b1, b0], r2.at[0], over_x), (g.at[1 - b2, b1, b0], r2.at[1], over_y),
                     (g.at[1 - b2, 1 - b1, b0], r3, across)]
            self.step(moves, [m[1] for m in moves], lambda: add_into(own, r2.at[0], r2.at[1], r3))
        elif kind[0] == "x":
            self.step([(g.at[:, 1 - b1, b0], r2, over_x)], [r2], lambda: self.fold_x(g, r2, b1, b0))
            self.step([(g.at[1 - b2, b1, b0], r3, over_y)], [r3], lambda: add_into(own, r3))
        else:
            self.step([(g.at[1 - b2, :, b0], r2, over_y)], [r2], lambda: self.fold_y(g, r2, b2, b0))
            self.step([(g.at[b2, 1 - b1, b0], r3, over_x)], [r3], lambda: add_into(own, r3))
        if kind[1] == "s":
            slots = [r4.at[:, pl.ds(0, cols)], r4.at[:, pl.ds(cols, cols)], r5]
            there = [lax.rem(z + o, 4) for o in (1, 2, 3)]
            back = [lax.rem(z + 4 - o, 4) for o in (1, 2, 3)]
            moves = [(quarter(own, there[i]), slots[i], (d, there[i])) for i in range(3)]
            self.step(moves, slots, lambda: self.finish(quarter(own, z), quarter(self.out, z), slots))
            mine = quarter(self.out, z)
            self.step([(mine, mine, (d, one)) for one in there], [quarter(self.out, one) for one in back], None)
        else:
            z0, z1 = lax.rem(z, 2), lax.div(z, 2)
            mine, other = at(z0, rows), at(1 - z0, rows)
            left, right = at(z1, cols), at(1 - z1, cols)
            half = own.at[mine]
            one, two = (d, flip(z, 1)), (d, flip(z, 2))
            self.step([(own.at[other], r4, one)], [r4], lambda: add_into(half, r4))
            self.step(
                [(own.at[mine, right], r5, two)], [r5],
                lambda: self.finish(own.at[mine, left], self.out.at[mine, left], [r5]),
            )
            done = self.out.at[mine, left]
            self.step([(done, done, two)], [self.out.at[mine, right]], None)
            done = self.out.at[mine]
            self.step([(done, done, one)], [self.out.at[other]], None)

    def step(self, moves, landing, combine):
        first = self.used
        self.used += len(moves)
        copies = [
            pltpu.make_async_remote_copy(
                src, dst, self.send.at[self.index, first + i], self.recv.at[self.index, first + i],
                device_id=to, device_id_type=MESH,
            )
            for i, (src, dst, to) in enumerate(moves)
        ]
        waits = [
            pltpu.make_async_copy(here, here, self.recv.at[self.index, first + i])
            for i, here in enumerate(landing)
        ]
        self.stages.append((copies, waits, combine))

    def fold(self, g, r, b0):
        @pl.loop(0, 4)
        def _(i):
            y, x = lax.div(i, 2), lax.rem(i, 2)
            add_into(g.at[y, x, b0], r.at[y, x])

    def fold_x(self, g, r, b1, b0):
        @pl.loop(0, 2)
        def _(i):
            add_into(g.at[i, b1, b0], r.at[i])

    def fold_y(self, g, r, b2, b0):
        @pl.loop(0, 2)
        def _(i):
            add_into(g.at[b2, i, b0], r.at[i])

    def finish(self, own, out, parts):
        total = own[...].astype(F32)
        for one in parts:
            total = total + one[...].astype(F32)
        out[...] = total.astype(out.dtype)

    def start(self):
        for copy in self.stages[0][0]:
            copy.start()

    def take(self, stage):
        _, waits, combine = self.stages[stage]
        for one in waits:
            one.wait()
        if combine is not None:
            combine()
        if stage + 1 < len(self.stages):
            for copy in self.stages[stage + 1][0]:
                copy.start()

    def ends(self, stage):
        return stage + 1 == len(self.stages)

    def close(self):
        for copies, _, _ in self.stages:
            for copy in copies:
                copy.wait_send()


KINDS = ("xs", "yh", "xh", "yh", "xh", "xs", "xh", "ys", "dh", "dh", "dh", "ds")
EARLY = 9
UNITS = 12
VECTORS, LOUT, GRAD = 12, 13, 15
SCHEDULE = (
    ((13, 0),),
    ((0, 0), (14, 0)),
    ((1, 0),),
    (),
    (),
    ((2, 0),),
    ((3, 0),),
    (),
    (),
    ((1, 1),),
    ((0, 1),),
    ((5, 0),),
    ((2, 1),),
    ((7, 0),),
    (),
    ((0, 3), (3, 2)),
    ((5, 2), (6, 0)),
    ((7, 2), (10, 0)),
    ((3, 4), (4, 2)),
    ((1, 2), (0, 2), (3, 1)),
    ((2, 2), (1, 3), (5, 1), (4, 0)),
    ((2, 3), (1, 4), (7, 1)),
    ((2, 4), (0, 4), (3, 3), (1, 5), (4, 1)),
    ((5, 3), (2, 5), (1, 6)),
    ((7, 3),),
    ((15, 0), (2, 6), (5, 4), (3, 5), (4, 3), (6, 1)),
)
TAIL = (
    (16, 0), (9, 0), (8, 0), (11, 0), (12, 0), (10, 1), (7, 4), (6, 2), (3, 6), (9, 1),
    (4, 4), (8, 1), (10, 2), (6, 3), (9, 2), (4, 5), (12, 1), (8, 2), (11, 1), (10, 3),
    (6, 4), (9, 3), (12, 2), (4, 6), (8, 3), (11, 2), (10, 4), (6, 5), (12, 3), (9, 4),
    (8, 4), (10, 5), (11, 3), (6, 6), (9, 5), (12, 4), (8, 5),
)
HEAD_ROWS = 16
STEP = 768


def sds(shape, dtype):
    return jax.ShapeDtypeStruct(shape, dtype)


def norm_parts(v):
    cen = v - jnp.mean(v, axis=-1, keepdims=True)
    inv = lax.rsqrt(jnp.mean(cen * cen, axis=-1, keepdims=True) + EPS)
    return cen * inv, inv


def norm_back(raw, unit, inv, gain):
    g = raw * gain
    return inv * (
        g - jnp.mean(g, axis=-1, keepdims=True) - unit * jnp.mean(g * unit, axis=-1, keepdims=True)
    )


class Return:
    def __init__(self, i, *refs):
        self.i, self.refs = i, refs

    def take(self, stage):
        swap_one(self.i, *self.refs)


class VectorSum:
    def __init__(self, sm, sr, send, recv, partners):
        self.sm, self.sr = sm, sr
        self.copies = [
            pltpu.make_async_remote_copy(
                sm.at[i % 2], sr.at[i], send.at[i], recv.at[i], device_id=to, device_id_type=MESH
            )
            for i, to in enumerate(partners)
        ]

    def start(self):
        self.copies[0].start()

    def take(self, i):
        self.copies[i].wait_recv()
        if i:
            self.copies[i - 1].wait_send()
        self.sm[(i + 1) % 2] = self.sm[i % 2] + self.sr[i]
        if i + 1 < len(self.copies):
            self.copies[i + 1].start()

    def close(self):
        self.copies[-1].wait_send()


def layer_kernel(
    bits,
    ts, buckets, x, cot, table, wm, wo, wu, wd, gains, shifts, biases, upb,
    lhome, ihome, f_out, total_out,
    xr, cr, embs, embr, kv, dkvr, r1, r2, r3, r4, r5, f, sm, sr,
    low1, q2, mixed, do, gm, lov, g, ls, lst, dt, upg, upv,
    xsend, xrecv, csend, crecv, esend, erecv, ksend, krecv, lsend, lrecv, isend, irecv,
    dsend, drecv, rsend, rrecv, ssend, srecv, wsem, osem,
):
    d, z, c, k = place()
    toks, width = xr.shape
    part = toks // 2
    ff = wu.shape[1]
    blk = toks // 2
    outer = (1 << len(bits)) // 8
    partner = flip(d, 1)
    row_of = lambda ref, i: ref[i : i + 1, :].astype(F32)
    load = lambda i, src, dst: pltpu.make_async_copy(src, dst, wsem.at[i])
    x_at, c_at = lambda s: xr.at[at(s, part)], lambda s: cr.at[at(s, part)]
    l_at = lambda s: lov.at[at(s, part)]
    low_half = iota((1, PAIR), 1) < HEAD_SIZE
    high_half = jnp.logical_not(low_half)
    lane = iota((1, PAIR), 1)
    mine = at(c, toks)

    across = (flip(flip(d, 2 * outer), 4 * outer), z)
    upv[0, :] = upb[...].astype(F32)
    greet(column_peers() + [(flip(d, bit), z) for bit in bits if bit > 1] + [across])
    swap_start(lambda i: x.at[i], x_at, xsend, xrecv)
    refs = (r1, r2, r3, r4, r5, f, rsend, rrecv)
    units = {i: Reduction(i, KINDS[i], g.at[i], refs, outer) for i in range(EARLY)}
    for i in range(2):
        units[LOUT + i] = Return(i, l_at, lambda s: lhome.at[s], lsend, lrecv)
    plan = iter(SCHEDULE)

    def point():
        for one, stage in next(plan):
            units[one].take(stage)

    def points(count, index):
        for i, row in enumerate([next(plan) for _ in range(count)]):
            if row:

                @pl.when(index == i)
                def _():
                    for one, stage in row:
                        units[one].take(stage)

    def kv_copy(p):
        return pltpu.make_async_remote_copy(
            kv.at[p, :, mine], kv.at[p, :, mine], ksend.at[p], krecv.at[p],
            device_id=(partner, z), device_id_type=MESH,
        )

    def project(wmv, tabv):
        load(1, wm, wmv).start()
        load(0, table, tabv).start()
        load(0, table, tabv).wait()
        row, col = iota((16, tabv.shape[0]), 0), iota((16, tabv.shape[0]), 1)
        wanted = jnp.where(row == 0, ts[0], ts[1])
        hits = jnp.where(jnp.logical_and(col == wanted, row < 2), 1.0, 0.0).astype(BF)
        picked = mm(hits, tabv[...])
        for i in range(2):
            embs[i] = jnp.broadcast_to(picked[i : i + 1], (16, width)).astype(BF)
        swap_start(lambda i: embs.at[i], lambda s: embr.at[s], esend, erecv)
        for s in range(2):
            swap_wait(lambda s: embr.at[s], erecv, s)
        gain, shift = row_of(gains, 0), row_of(shifts, 0)
        for s in range(2):
            swap_wait(x_at, xrecv, s)
            emb = embr[s][0:1, :].astype(F32)

            @pl.loop(0, part // 128)
            def _(b):
                rows = pl.ds(pl.multiple_of(s * part + b * 128, 128), 128)
                unit, _ = norm_parts(xr[rows, :].astype(F32) + emb)
                low1[rows, :] = (unit * gain + shift).astype(BF)

        swap_start(lambda i: cot.at[i], c_at, csend, crecv)
        load(1, wm, wmv).wait()

        @pl.loop(0, PAIRS // 2)
        def _(i):
            res = mm(low1[...], wmv[:, at(i, 6 * PAIR)])
            for j in range(2):
                p = 2 * i + j
                t0, t1, t2 = (res[:, (3 * j + n) * PAIR : (3 * j + n + 1) * PAIR] for n in range(3))
                q2[p] = (jnp.where(low_half, t0, t1).astype(BF) * 0.125).astype(BF)
                kv[p, 0, mine, :] = pltpu.roll(jnp.where(low_half, t2, t0), HEAD_SIZE, 1).astype(BF)
                kv[p, 1, mine, :] = jnp.where(low_half, t1, t2).astype(BF)
                kv_copy(p).start()

    def attend():
        @pl.loop(0, PAIRS)
        def _(p):
            kv_copy(p).wait_recv()
            q, keys, vals = q2[p], kv[p, 0], kv[p, 1]
            scores = [mm_nt(jnp.where(half, q, jnp.zeros_like(q)), keys) for half in (low_half, high_half)]
            tops = [jnp.max(s, axis=-1, keepdims=True) for s in scores]
            powers = [jnp.exp(s - top) for s, top in zip(scores, tops)]
            lows = [e.astype(BF) for e in powers]
            totals = [jnp.sum(e, axis=-1, keepdims=True) for e in powers]
            outs = [mm(e, vals) * (1.0 / total) for e, total in zip(lows, totals)]
            sums = [top + jnp.log(total) for top, total in zip(tops, totals)]
            mixed[:, at(p, PAIR)] = jnp.where(low_half, *outs).astype(BF)
            ls[...] = jnp.where(lane == 2 * p, sums[0], jnp.where(lane == 2 * p + 1, sums[1], ls[...]))

        lst[...] = ls[...].T

    def feed(wov, wuv, wdv, mid, low2, low2t, hid, rl):
        load(2, wo, wov).wait()
        gain, shift, bias = row_of(gains, 1), row_of(shifts, 1), row_of(biases, 0)

        @pl.loop(0, 2)
        def _(b):
            rows = at(b, blk)
            v = xr[rows, :].astype(F32) + embr[b][0:1, :].astype(F32)
            v = v + mm(mixed[rows, :], wov[...]) + bias
            mid[rows, :] = v
            low2[rows, :] = (norm_parts(v)[0] * gain + shift).astype(BF)

        low2t[...] = low2[...].T
        load(3, wu, wuv).wait()

        @pl.loop(0, ff // STEP)
        def _(j):
            cols = at(j, STEP)
            r = mm(low2[...], wuv[:, cols]) + upv[:, cols]
            half = 0.5 * (1.0 + lax.erf(r * math.sqrt(0.5)))
            bell = jnp.exp(r * r * -0.5) * (1.0 / math.sqrt(2.0 * math.pi))
            hid[:, cols] = (r * half).astype(BF)
            rl[:, cols] = (half + r * bell).astype(BF)

        load(4, wd, wdv).wait()
        for s in range(2):
            swap_wait(c_at, crecv, s)
        n = g.shape[-2]

        @pl.loop(0, 4)
        def _(j):
            res = mm_tn(hid[:, at(j, width)], cr[...]).astype(BF)
            for s in range(2):
                for i in range(4):
                    first = (4 * s + i) * n
                    g[i, lax.div(j, 2), lax.rem(j, 2), s] = res[first : first + n]

        for i in range(4):
            units[i].start()
        fin = mid[...] + mm(hid[...], wdv[...]) + row_of(biases, 1)
        lov[...] = fin.astype(BF)
        sm[0, 8:9, :] = jnp.sum(fin * fin, axis=0, keepdims=True)
        point()

        @pl.loop(0, ff // STEP)
        def _(j):
            cols = at(j, STEP)
            low = (mm_nt(cr[...], wdv[cols, :]) * rl[:, cols].astype(F32)).astype(BF)
            rl[:, cols] = low
            upg[:, cols] = jnp.sum(low.astype(F32), axis=0, keepdims=True)
            points(4, j)


        @pl.loop(0, 4)
        def _(j):
            res = mm(low2t[...], rl[:, at(j, width)]).astype(BF)
            for i in range(8):
                g[4 + j, i // 4, (i // 2) % 2, i % 2] = res[i * n : (i + 1) * n]
            for i in range(4):

                @pl.when(j == i)
                def _():
                    units[4 + i].start()

            points(4, j)

        gm[...] = mm_nt(rl[...], wuv[...])
        point()

        @pl.loop(0, toks // 128)
        def _(b):
            rows = at(b, 128)
            unit, inv = norm_parts(mid[rows, :])
            raw = gm[rows, :]
            ct = cr[rows, :].astype(F32)
            grad = ct + norm_back(raw, unit, inv, gain)
            gm[rows, :] = grad
            sm[0, 0:1, :] += jnp.sum(raw * unit, axis=0, keepdims=True)
            sm[0, 1:2, :] += jnp.sum(raw, axis=0, keepdims=True)
            sm[0, 2:3, :] += jnp.sum(grad.astype(BF).astype(F32), axis=0, keepdims=True)
            sm[0, 3:4, :] += jnp.sum(ct, axis=0, keepdims=True)

        for i in range(4):
            sm[0, 4 + i : 5 + i, :] = upg[:, i * width : (i + 1) * width]
        point()
        res = mm_tn(mixed[...], gm[...].astype(BF)).astype(BF)
        for i in range(8):
            g[8, i // 4, (i // 2) % 2, i % 2] = res[i * n : (i + 1) * n]
        units[8].start()
        point()
        fold = lax.div(iota((PAIR, width), 1), HEAD_SIZE) == iota((PAIR, width), 0)
        fold = jnp.where(fold, 1.0, 0.0).astype(BF)
        dout = mm_nt(gm[...].astype(BF), wov[...]).astype(BF)
        do[...] = dout
        prod = dout.astype(F32) * mixed[...].astype(F32)
        high = prod.astype(BF)
        rest = (prod - high.astype(F32)).astype(BF)
        dt[...] = mm_nt(fold, high) + mm_nt(fold, rest)
        point()

    def forward(wov, wuv, wdv):
        load(2, wo, wov).start()
        load(3, wu, wuv).start()
        load(4, wd, wdv).start()
        sm[0] = jnp.zeros_like(sm[0])
        pl.run_scoped(project, pltpu.VMEM(wm.shape, BF), pltpu.VMEM(table.shape, BF))
        attend()
        pl.run_scoped(
            functools.partial(feed, wov, wuv, wdv),
            pltpu.VMEM((toks, width), F32), pltpu.VMEM((toks, width), BF), pltpu.VMEM((width, toks), BF),
            pltpu.VMEM((toks, ff), BF), pltpu.VMEM((toks, ff), BF),
        )

    pl.run_scoped(forward, pltpu.VMEM(wo.shape, BF), pltpu.VMEM(wu.shape, BF), pltpu.VMEM(wd.shape, BF))

    def backward(wmv, low1t, late_g, dkvs, dqa, dqkv, igv):
        load(5, wm, wmv).start()
        low1t[...] = low1[...].T
        for i in range(EARLY, UNITS):
            units[i] = Reduction(i, KINDS[i], late_g.at[i - EARLY], refs, outer)
        i_at = lambda s: igv.at[at(s, part)]

        def dkv_copy(p):
            return pltpu.make_async_remote_copy(
                dkvs.at[p], dkvr.at[p], dsend.at[p], drecv.at[p],
                device_id=(partner, z), device_id_type=MESH,
            )

        halves = (low_half, high_half)

        def attend_back(p, base):
            rows = pl.ds(pl.multiple_of(base, toks), toks)
            keys, vals = kv[p, 0, rows, :], kv[p, 1, rows, :]
            q, dout = q2[p], do[:, at(p, PAIR)]
            dks, dvs, dqs = [], [], []
            for h, half in enumerate(halves):
                kh = jnp.where(half, keys, jnp.zeros_like(keys))
                vh = jnp.where(half, vals, jnp.zeros_like(vals))
                probs = jnp.exp(mm_nt(kh, q) - lst[pl.ds(2 * p + h, 1), :])
                ds = (probs * (mm_nt(vh, dout) - dt[pl.ds(2 * p + h, 1), :])).astype(BF)
                dvs.append(mm(probs.astype(BF), dout))
                dks.append(mm(ds, q))
                dqs.append(mm_tn(ds, kh))
            return jnp.where(low_half, *dks), jnp.where(low_half, *dvs), dqs[0] + dqs[1]

        @pl.loop(0, PAIRS)
        def _(p):
            dk, dv, dq = attend_back(p, (1 - c) * toks)
            dkvs[p, 0] = dk.astype(BF)
            dkvs[p, 1] = dv.astype(BF)
            dqa[...] = dq
            dkv_copy(p).start()
            points(PAIRS, p)
            dk, dv, dq = attend_back(p, c * toks)
            dkv_copy(p).wait_recv()
            dq = (dq + dqa[...]) * 0.125
            dk = pltpu.roll(dk + dkvr[p, 0].astype(F32), HEAD_SIZE, 1)
            dv = dv + dkvr[p, 1].astype(F32)
            dqkv[:, at(3 * p, PAIR)] = jnp.where(low_half, dq, dk).astype(BF)
            dqkv[:, at(3 * p + 1, PAIR)] = jnp.where(low_half, dv, dq).astype(BF)
            dqkv[:, at(3 * p + 2, PAIR)] = jnp.where(low_half, dk, dv).astype(BF)

            @pl.when(lax.rem(p, 2) == 1)
            def _():
                b = lax.div(p, 2)
                n = g.shape[-2]
                res = mm(low1t[...], dqkv[:, at(b, width)]).astype(BF)
                for j in range(8):
                    late_g[b, j // 4, (j // 2) % 2, j % 2] = res[j * n : (j + 1) * n]
                for i in range(3):

                    @pl.when(b == i)
                    def _():
                        units[EARLY + i].start()

            points(PAIRS, p)

        load(5, wm, wmv).wait()
        gain0 = row_of(gains, 0)
        here = 4 * k + z
        lanes = iota((1, width), 1)

        @pl.loop(0, 2)
        def _(b):
            rows = at(b, blk)
            raw = mm_nt(dqkv[rows, :], wmv[...])
            unit, inv = norm_parts(xr[rows, :].astype(F32) + embr[b][0:1, :].astype(F32))
            grad = gm[rows, :] + norm_back(raw, unit, inv, gain0)
            igv[rows, :] = grad.astype(BF)
            sm[0, 11:12, :] += jnp.sum(raw * unit, axis=0, keepdims=True)
            sm[0, 12:13, :] += jnp.sum(raw, axis=0, keepdims=True)
            sm[0, 13:14, :] += jnp.sum(grad, axis=0, keepdims=True)

        square = jnp.sum(sm[0, 8:9, :]) * (1.0 / (2 * toks * width))
        sm[0, 8:9, :] = jnp.where(lanes == here, square, 0.0)
        for row, source in ((9, ts), (10, buckets)):
            first, second = source[0].astype(F32), source[1].astype(F32)
            line = jnp.where(lanes == 2 * d, first, jnp.where(lanes == 2 * d + 1, second, 0.0))
            sm[0, row : row + 1, :] = jnp.where(z == 0, line, jnp.zeros_like(line))
        sums = sm.shape[1] - HEAD_ROWS
        sm[0, HEAD_ROWS:, :] = jnp.where(iota((sums, 1), 0) == here, sm[0, 13:14, :], 0.0)
        stages = [(flip(d, bit), z) for bit in bits] + [(d, flip(z, 1)), (d, flip(z, 2))]

        vectors = VectorSum(sm, sr, ssend, srecv, stages)
        units[VECTORS] = vectors
        for i in range(2):
            units[GRAD + i] = Return(i, i_at, lambda s: ihome.at[s], isend, irecv)
        vectors.start()

        def put(i):
            return pltpu.make_async_copy(f.at[i], f_out.at[i], osem.at[i])

        point()
        for one, stage in TAIL:
            units[one].take(stage)
            if one < UNITS and units[one].ends(stage):
                put(one).start()
        for one in range(UNITS):
            if not any(i == one and units[one].ends(stage) for i, stage in TAIL):
                put(one).start()
        extra = len(stages) - 5
        for i in range(extra):
            vectors.take(5 + i)
        result = pltpu.make_async_copy(sm.at[len(stages) % 2], total_out, wsem.at[0])
        result.start()
        for i in range(UNITS + 1):
            units[i].close()
        for i in range(UNITS):
            put(i).wait()
        result.wait()

        @pl.loop(0, PAIRS)
        def _(p):
            kv_copy(p).wait_send()
            dkv_copy(p).wait_send()

        for s in range(2):
            swap_wait(lambda s: lhome.at[s], lrecv, s)
            swap_wait(lambda s: ihome.at[s], irecv, s)
        swap_sent(lambda i: x.at[i], x_at, xsend, xrecv)
        swap_sent(lambda i: cot.at[i], c_at, csend, crecv)
        swap_sent(lambda i: embs.at[i], lambda s: embr.at[s], esend, erecv)
        swap_sent(l_at, lambda s: lhome.at[s], lsend, lrecv)
        swap_sent(i_at, lambda s: ihome.at[s], isend, irecv)

    shard = g.shape[-2]
    pl.run_scoped(
        backward,
        pltpu.VMEM(wm.shape, BF), pltpu.VMEM((width, toks), BF),
        pltpu.VMEM((UNITS - EARLY, 2, 2, 2, shard, width), BF), pltpu.VMEM((PAIRS, 2, toks, PAIR), BF),
        pltpu.VMEM((toks, PAIR), F32), pltpu.VMEM((toks, 3 * width), BF),
        pltpu.VMEM((toks, width), BF),
    )


def run_layer(ts, buckets, x, cot, table, wm, wo, wu, wd, gains, shifts, biases, upb, dp):
    _, part, width = x.shape
    toks = 2 * part
    ff = wu.shape[1]
    shard = width // 8
    bits = axis_bits(dp)
    rows = HEAD_ROWS + 2 * dp
    stages = len(bits) + 2
    vm = lambda shape, dtype: pltpu.VMEM(shape, dtype)
    any_ = pl.BlockSpec(memory_space=pl.ANY)
    vmem = pl.BlockSpec(memory_space=pltpu.VMEM)
    smem = pl.BlockSpec(memory_space=pltpu.SMEM)
    dma = lambda *n: pltpu.SemaphoreType.DMA(n)
    return pl.pallas_call(
        functools.partial(layer_kernel, bits),
        out_shape=(
            sds((2, part, width), BF), sds((2, part, width), BF), sds((UNITS, shard, width), BF),
            sds((rows, width), F32),
        ),
        in_specs=[smem] * 2 + [any_] * 7 + [vmem] * 4,
        out_specs=(any_,) * 4,
        scratch_shapes=[
            vm((toks, width), BF), vm((toks, width), BF), vm((2, 16, width), BF), vm((2, 16, width), BF),
            vm((PAIRS, 2, 2 * toks, PAIR), BF), vm((PAIRS, 2, toks, PAIR), BF),
            vm((UNITS, 2, 2, shard, width), BF), vm((UNITS, 2, shard, width), BF), vm((UNITS, shard, width), BF),
            vm((UNITS, shard // 2, width), BF), vm((UNITS, shard // 2, width // 2), BF),
            vm((UNITS, shard, width), BF), vm((2, rows, width), F32), vm((stages, rows, width), F32),
            vm((toks, width), BF), vm((PAIRS, toks, PAIR), BF), vm((toks, width), BF), vm((toks, width), BF),
            vm((toks, width), F32), vm((toks, width), BF), vm((EARLY, 2, 2, 2, shard, width), BF),
            vm((toks, PAIR), F32), vm((PAIR, toks), F32), vm((PAIR, toks), F32), vm((1, ff), F32), vm((1, ff), F32),
            dma(2), dma(2), dma(2), dma(2), dma(2), dma(2), dma(PAIRS), dma(PAIRS),
            dma(2), dma(2), dma(2), dma(2), dma(PAIRS), dma(PAIRS), dma(UNITS, 10), dma(UNITS, 10),
            dma(stages), dma(stages), dma(6), dma(UNITS),
        ],
        compiler_params=pltpu.CompilerParams(
            collective_id=0, has_side_effects=True, vmem_limit_bytes=127 << 19
        ),
        cost_estimate=pl.CostEstimate(
            flops=32_000_000_000, bytes_accessed=60_000_000, transcendentals=20_000_000
        ),
        name="layer",
    )(ts, buckets, x, cot, table, wm, wo, wu, wd, gains, shifts, biases, upb)


def finish_kernel(
    lhome, ihome_in, f_in, total_in, *refs,
):
    big, small, held = refs[:7], refs[7:13], refs[13:20]
    layer_out, input_grad, mixer, output, up, down, table = held
    gains, shifts, biases, upb, norms, counts = small
    ihome, f, total, sem, done = refs[20:]
    n, width = f.shape[1:]
    columns, step_count = table.shape
    copies = [pltpu.make_async_copy(total_in, total, sem.at[0])]
    copies += [
        pltpu.make_async_copy(f_in.at[pl.ds(4 * i, 4)], f.at[pl.ds(4 * i, 4)], sem.at[1 + i]) for i in range(3)
    ]
    copies += [pltpu.make_async_copy(ihome_in, ihome, sem.at[4]), pltpu.make_async_copy(lhome, layer_out, sem.at[5])]
    for one in copies:
        one.start()
    leave = [pltpu.make_async_copy(src, dst, done.at[i]) for i, (src, dst) in enumerate(zip(held, big))]
    copies[1].wait()
    for i in range(4):
        down[i * n : (i + 1) * n, :] = f[i].astype(F32)
    leave[5].start()
    copies[2].wait()
    for i in range(4):
        up[:, i * width : (i + 1) * width] = f[4 + i].astype(F32)
    leave[4].start()
    copies[4].wait()
    input_grad[...] = ihome[...].astype(F32)
    leave[1].start()
    copies[3].wait()
    output[...] = f[8].astype(F32)
    for i in range(3):
        mixer[:, i * width : (i + 1) * width] = f[9 + i].astype(F32)
    leave[3].start()
    leave[2].start()
    copies[5].wait()
    leave[0].start()
    copies[0].wait()
    for i in range(4):
        upb[pl.ds(i * width, width)] = total[4 + i, :]
    for i, row in enumerate((11, 0)):
        gains[i : i + 1, :] = total[row : row + 1, :]
        shifts[i : i + 1, :] = total[row + 1 : row + 2, :]
    biases[...] = total[2:4, :]
    count = total.shape[0] - HEAD_ROWS
    first = lax.axis_index("dp") * columns
    chosen = iota((width, columns), 0) == iota((width, columns), 1) + first
    chosen = jnp.where(chosen, 1.0, 0.0).astype(BF)
    steps = total[9:10, :count]
    hits = jnp.where(iota((step_count, count), 0).astype(F32) == steps, 1.0, 0.0).astype(BF)
    here = iota((BUCKETS, count), 0).astype(F32) == total[10:11, :count]
    here = jnp.where(here, 1.0, 0.0).astype(BF)
    rest, grad = total[HEAD_ROWS:, :], 0.0
    means = jnp.where(iota((8, count), 0) == 0, total[8:9, :count], 1.0)
    norm = 0.0
    for _ in range(3):
        piece = rest.astype(BF)
        rest = rest - piece.astype(F32)
        part = mm(piece, chosen).astype(BF)
        grad = grad + lax.dot_general(part, hits, (((0,), (1,)), ((), ())), preferred_element_type=F32)
        piece = means.astype(BF)
        means = means - piece.astype(F32)
        norm = norm + mm_nt(piece, here)
    table[...] = grad
    leave[6].start()
    norms[...] = norm[0, :]
    counts[...] = norm[1, :]
    for one in leave:
        one.wait()


def run_finish(lhome, ihome, f, total, dp, steps):
    n, width = f.shape[1:]
    big = [
        sds(lhome.shape, BF), sds(ihome.shape, F32), sds((n, 3 * width), F32), sds((n, width), F32),
        sds((n, 4 * width), F32), sds((4 * n, width), F32), sds((width // dp, steps), F32),
    ]
    small = [sds((2, width), F32)] * 3 + [sds((4 * width,), F32), sds((BUCKETS,), F32), sds((BUCKETS,), F32)]
    vmem, any_ = pl.BlockSpec(memory_space=pltpu.VMEM), pl.BlockSpec(memory_space=pl.ANY)
    res = pl.pallas_call(
        finish_kernel,
        out_shape=big + small,
        in_specs=[any_] * 4,
        out_specs=[any_] * len(big) + [vmem] * len(small),
        scratch_shapes=[pltpu.VMEM(one.shape, one.dtype) for one in big] + [
            pltpu.VMEM(ihome.shape, BF), pltpu.VMEM(f.shape, f.dtype), pltpu.VMEM(total.shape, F32),
            pltpu.SemaphoreType.DMA((6,)), pltpu.SemaphoreType.DMA((len(big),)),
        ],
        compiler_params=pltpu.CompilerParams(vmem_limit_bytes=60 << 20),
        name="finish",
    )(lhome, ihome, f, total)
    return (*res[:6], *res[7:11], res[6].T, *res[11:])


def body(
    inputs, cotangent, time_table, timesteps, buckets, mixer_weight, output_weight, up_weight, down_weight,
    norm_gain, norm_shift, output_bias, up_bias,
):
    width = inputs.shape[-1]
    dp = lax.axis_size("dp")
    lhome, ihome, shares, total = run_layer(
        timesteps, buckets, inputs, cotangent, time_table, mixer_weight, output_weight, up_weight,
        down_weight, norm_gain, norm_shift, output_bias, up_bias, dp,
    )
    inner = dp // 8
    if inner > 1:
        teams = [[h * inner + i for i in range(inner)] for h in range(8)]
        scatter = lambda a, axis: lax.psum_scatter(
            a, "dp", scatter_dimension=axis, axis_index_groups=teams, tiled=True
        )
        shares = shares.astype(F32)
        down, rest = scatter(shares[0:4].reshape(width // 2, width), 0), scatter(shares[4:UNITS], 1)
        shares = jnp.concatenate([down.reshape((4,) + rest.shape[1:]), rest])
    return run_finish(lhome, ihome, shares, total, dp, time_table.shape[0])


def solution(mesh):
    tokens = P("dp", "seq", None)
    return jax.shard_map(
        body,
        mesh=mesh,
        in_specs=(tokens, tokens, P(), P("dp"), P("dp")) + (P(),) * 8,
        out_specs=(tokens, tokens) + (P("dp", None),) * 4 + (P(),) * 4 + (P(None, "dp"), P(), P()),
        check_vma=False,
    )
```

```python
import functools
import math

import jax
import jax.numpy as jnp
from jax import lax
from jax.experimental import pallas as pl
from jax.experimental.pallas import tpu as pltpu
from jax.sharding import PartitionSpec as P

HEADS = 12
HEAD_SIZE = 64
PAIRS = HEADS // 2
PAIR = 2 * HEAD_SIZE
STEPS = 2000
BUCKETS = 8
EPS = 1e-05

BF = jnp.bfloat16
F32 = jnp.float32
MESH = pl.DeviceIdType.MESH


def mm(a, b):
    return lax.dot_general(a, b, (((1,), (0,)), ((), ())), preferred_element_type=F32)


def mm_nt(a, b):
    return lax.dot_general(a, b, (((1,), (1,)), ((), ())), preferred_element_type=F32)


def mm_tn(a, b):
    return lax.dot_general(a, b, (((0,), (0,)), ((), ())), preferred_element_type=F32)


def iota(shape, axis):
    return lax.broadcasted_iota(jnp.int32, shape, axis)


def place():
    d, z = lax.axis_index("dp"), lax.axis_index("seq")
    return d, z, lax.rem(d, 2), lax.div(d, 2)


def column_peers():
    d, z, c, k = place()
    found = []
    for off in range(1, 8):
        m = lax.rem(c * 4 + z + off, 8)
        found.append((2 * k + lax.div(m, 4), lax.rem(m, 4)))
    return found


def greet(ids):
    barrier = pltpu.get_barrier_semaphore()
    for one in ids:
        pl.semaphore_signal(barrier, inc=1, device_id=one, device_id_type=MESH)
    pl.semaphore_wait(barrier, len(ids))


def swap_part(i):
    d, z, c, k = place()
    core, chip = lax.div(z, 2), 2 * c + i
    return core, chip, jnp.logical_and(core == c, chip == z), 2 * k + core


def swap_one(i, source, target, send, recv):
    slot = lax.rem(lax.axis_index("seq"), 2)
    core, chip, own, there = swap_part(i)

    @pl.when(own)
    def _():
        pltpu.make_async_copy(source(i), target(slot), recv.at[slot]).start()

    @pl.when(jnp.logical_not(own))
    def _():
        pltpu.make_async_remote_copy(
            source(i), target(slot), send.at[i], recv.at[slot],
            device_id=(there, chip), device_id_type=MESH,
        ).start()


def swap_start(source, target, send, recv):
    for i in range(2):
        swap_one(i, source, target, send, recv)


def swap_wait(target, recv, s):
    pltpu.make_async_copy(target(s), target(s), recv.at[s]).wait()


def swap_sent(source, target, send, recv):
    for i in range(2):
        core, chip, own, there = swap_part(i)

        @pl.when(jnp.logical_not(own))
        def _():
            pltpu.make_async_remote_copy(
                source(i), target(i), send.at[i], recv.at[i],
                device_id=(there, chip), device_id_type=MESH,
            ).wait_send()


def at(i, n):
    return pl.ds(pl.multiple_of(i * n, n), n)


def flip(index, bit):
    return index + bit - 2 * bit * lax.rem(lax.div(index, bit), 2)


def bit_of(index, bit):
    return lax.rem(lax.div(index, bit), 2)


def axis_bits(size):
    found, bit = [], 1
    while bit < size:
        found.append(bit)
        bit *= 2
    return found


def add_into(dst, *parts):
    total = dst[...].astype(F32)
    for one in parts:
        total = total + one[...].astype(F32)
    dst[...] = total.astype(dst.dtype)


class Reduction:
    def __init__(self, index, kind, g, refs, outer):
        self.index, self.kind, self.g = index, kind, g
        r1, r2, r3, r4, r5, out, self.send, self.recv = refs
        self.out = out.at[index]
        r1, r2, r3, r4, r5 = (r.at[index] for r in (r1, r2, r3, r4, r5))
        d, z, _, _ = place()
        b0, b1, b2 = bit_of(d, outer), bit_of(d, 2 * outer), bit_of(d, 4 * outer)
        near, over_x, over_y = (flip(d, outer), z), (flip(d, 2 * outer), z), (flip(d, 4 * outer), z)
        across = (flip(flip(d, 2 * outer), 4 * outer), z)
        rows, cols = g.shape[-2] // 2, g.shape[-1] // 2
        own = g.at[b2, b1, b0]
        self.used, self.stages = 0, []

        def quarter(ref, q):
            return ref.at[at(lax.rem(q, 2), rows), at(lax.div(q, 2), cols)]

        self.step([(g.at[:, :, 1 - b0], r1, near)], [r1], lambda: self.fold(g, r1, b0))
        if kind[0] == "d":
            moves = [(g.at[b2, 1 - b1, b0], r2.at[0], over_x), (g.at[1 - b2, b1, b0], r2.at[1], over_y),
                     (g.at[1 - b2, 1 - b1, b0], r3, across)]
            self.step(moves, [m[1] for m in moves], lambda: add_into(own, r2.at[0], r2.at[1], r3))
        elif kind[0] == "x":
            self.step([(g.at[:, 1 - b1, b0], r2, over_x)], [r2], lambda: self.fold_x(g, r2, b1, b0))
            self.step([(g.at[1 - b2, b1, b0], r3, over_y)], [r3], lambda: add_into(own, r3))
        else:
            self.step([(g.at[1 - b2, :, b0], r2, over_y)], [r2], lambda: self.fold_y(g, r2, b2, b0))
            self.step([(g.at[b2, 1 - b1, b0], r3, over_x)], [r3], lambda: add_into(own, r3))
        if kind[1] == "s":
            slots = [r4.at[:, pl.ds(0, cols)], r4.at[:, pl.ds(cols, cols)], r5.at[:, pl.ds(0, cols)]]
            there = [lax.rem(z + o, 4) for o in (1, 2, 3)]
            back = [lax.rem(z + 4 - o, 4) for o in (1, 2, 3)]
            moves = [(quarter(own, there[i]), slots[i], (d, there[i])) for i in range(3)]
            self.step(moves, slots, lambda: self.finish(quarter(own, z), quarter(self.out, z), slots))
            mine = quarter(self.out, z)
            self.step([(mine, mine, (d, one)) for one in there], [quarter(self.out, one) for one in back], None)
        else:
            z0 = lax.rem(z, 2)
            mine, other = at(z0, rows), at(1 - z0, rows)
            half, done = own.at[mine], self.out.at[mine]
            one, two = (d, flip(z, 1)), (d, flip(z, 2))
            self.step([(own.at[other], r4, one)], [r4], lambda: add_into(half, r4))
            self.step([(half, r5, two)], [r5], lambda: self.finish(half, done, [r5]))
            self.step([(done, done, one)], [self.out.at[other]], None)

    def step(self, moves, landing, combine):
        first = self.used
        self.used += len(moves)
        copies = [
            pltpu.make_async_remote_copy(
                src, dst, self.send.at[self.index, first + i], self.recv.at[self.index, first + i],
                device_id=to, device_id_type=MESH,
            )
            for i, (src, dst, to) in enumerate(moves)
        ]
        waits = [
            pltpu.make_async_copy(here, here, self.recv.at[self.index, first + i])
            for i, here in enumerate(landing)
        ]
        self.stages.append((copies, waits, combine))

    def fold(self, g, r, b0):
        @pl.loop(0, 4)
        def _(i):
            y, x = lax.div(i, 2), lax.rem(i, 2)
            add_into(g.at[y, x, b0], r.at[y, x])

    def fold_x(self, g, r, b1, b0):
        @pl.loop(0, 2)
        def _(i):
            add_into(g.at[i, b1, b0], r.at[i])

    def fold_y(self, g, r, b2, b0):
        @pl.loop(0, 2)
        def _(i):
            add_into(g.at[b2, i, b0], r.at[i])

    def finish(self, own, out, parts):
        total = own[...].astype(F32)
        for one in parts:
            total = total + one[...].astype(F32)
        out[...] = total.astype(out.dtype)

    def start(self):
        for copy in self.stages[0][0]:
            copy.start()

    def take(self, stage):
        _, waits, combine = self.stages[stage]
        for one in waits:
            one.wait()
        if combine is not None:
            combine()
        if stage + 1 < len(self.stages):
            for copy in self.stages[stage + 1][0]:
                copy.start()

    def ends(self, stage):
        return stage + 1 == len(self.stages)

    def close(self):
        for copies, _, _ in self.stages:
            for copy in copies:
                copy.wait_send()


KINDS = ("xs", "ye", "xe", "ye", "xs", "ys", "xe", "ye", "ds", "de", "de", "de")
EARLY = 9
UNITS = 12
VECTORS, LOUT, GRAD = 12, 13, 15
SCHEDULE = (
    ((0, 0), (13, 0)),
    ((1, 0),),
    (),
    (),
    ((2, 0),),
    ((3, 0),),
    (),
    ((14, 0),),
    (),
    ((1, 1), (0, 1)),
    ((4, 0),),
    ((2, 1),),
    (),
    ((1, 2), (5, 0)),
    ((4, 1),),
    ((4, 2), (0, 4)),
    ((4, 3), (7, 1)),
    ((5, 3), (9, 0)),
    ((5, 4), (7, 3), (10, 0)),
    ((0, 2), (3, 1)),
    ((0, 3),),
    ((8, 0), (3, 3)),
    (),
    ((7, 2), (8, 1), (3, 5), (4, 4)),
    (),
    (),
    ((2, 3), (7, 0), (3, 2)),
    ((1, 5), (2, 4)),
    (),
    (),
    ((8, 2),),
    ((2, 2), (1, 3), (6, 0)),
    ((1, 4), (5, 1)),
    ((5, 2),),
    ((2, 5), (3, 4), (6, 1)),
    ((6, 2),),
    ((6, 3), (9, 1), (7, 4)),
    ((15, 0), (8, 3), (11, 0)),
)
TAIL = (
    (16, 0), (9, 2), (12, 0), (7, 5), (6, 4), (10, 1), (12, 1), (11, 1), (12, 2), (6, 5),
    (10, 2), (11, 2), (9, 3), (12, 3), (10, 3), (9, 4), (11, 3), (10, 4), (12, 4), (11, 4),
)
HEAD_ROWS = 16
STEP = 768


def sds(shape, dtype):
    return jax.ShapeDtypeStruct(shape, dtype)


def norm_parts(v):
    cen = v - jnp.mean(v, axis=-1, keepdims=True)
    inv = lax.rsqrt(jnp.mean(cen * cen, axis=-1, keepdims=True) + EPS)
    return cen * inv, inv


def norm_back(raw, unit, inv, gain):
    g = raw * gain
    return inv * (
        g - jnp.mean(g, axis=-1, keepdims=True) - unit * jnp.mean(g * unit, axis=-1, keepdims=True)
    )


class Return:
    def __init__(self, i, *refs):
        self.i, self.refs = i, refs

    def take(self, stage):
        swap_one(self.i, *self.refs)


class VectorSum:
    def __init__(self, sm, sr, send, recv, partners):
        self.sm, self.sr = sm, sr
        self.copies = [
            pltpu.make_async_remote_copy(
                sm.at[i % 2], sr.at[i], send.at[i], recv.at[i], device_id=to, device_id_type=MESH
            )
            for i, to in enumerate(partners)
        ]

    def start(self):
        self.copies[0].start()

    def take(self, i):
        self.copies[i].wait_recv()
        if i:
            self.copies[i - 1].wait_send()
        self.sm[(i + 1) % 2] = self.sm[i % 2] + self.sr[i]
        if i + 1 < len(self.copies):
            self.copies[i + 1].start()

    def close(self):
        self.copies[-1].wait_send()


def layer_kernel(
    bits,
    ts, buckets, x, cot, table, wm, wo, wu, wd, gains, shifts, biases, upb,
    lhome, ihome, f_out, total_out,
    xr, cr, embs, embr, kv, dkvr, r1, r2, r3, r4, r5, f, sm, sr,
    low1, q2, mixed, do, gm, lov, g, ls, lst, dt, upg, upv,
    xsend, xrecv, csend, crecv, esend, erecv, ksend, krecv, lsend, lrecv, isend, irecv,
    dsend, drecv, rsend, rrecv, ssend, srecv, wsem, osem,
):
    d, z, c, k = place()
    toks, width = xr.shape
    part = toks // 2
    ff = wu.shape[1]
    blk = toks // 2
    outer = (1 << len(bits)) // 8
    partner = flip(d, 1)
    row_of = lambda ref, i: ref[i : i + 1, :].astype(F32)
    load = lambda i, src, dst: pltpu.make_async_copy(src, dst, wsem.at[i])
    x_at, c_at = lambda s: xr.at[at(s, part)], lambda s: cr.at[at(s, part)]
    l_at = lambda s: lov.at[at(s, part)]
    low_half = iota((1, PAIR), 1) < HEAD_SIZE
    high_half = jnp.logical_not(low_half)
    lane = iota((1, PAIR), 1)
    mine = at(c, toks)

    across = (flip(flip(d, 2 * outer), 4 * outer), z)
    upv[0, :] = upb[...].astype(F32)
    greet(column_peers() + [(flip(d, bit), z) for bit in bits if bit > 1] + [across])
    swap_start(lambda i: x.at[i], x_at, xsend, xrecv)
    refs = (r1, r2, r3, r4, r5, f, rsend, rrecv)
    units = {i: Reduction(i, KINDS[i], g.at[i], refs, outer) for i in range(EARLY)}
    for i in range(2):
        units[LOUT + i] = Return(i, l_at, lambda s: lhome.at[s], lsend, lrecv)
    plan = iter(SCHEDULE)

    def point():
        for one, stage in next(plan):
            units[one].take(stage)

    def points(count, index):
        for i, row in enumerate([next(plan) for _ in range(count)]):
            if row:

                @pl.when(index == i)
                def _():
                    for one, stage in row:
                        units[one].take(stage)

    def kv_copy(p):
        return pltpu.make_async_remote_copy(
            kv.at[p, :, mine], kv.at[p, :, mine], ksend.at[p], krecv.at[p],
            device_id=(partner, z), device_id_type=MESH,
        )

    def project(wmv, tabv):
        load(1, wm, wmv).start()
        load(0, table, tabv).start()
        load(0, table, tabv).wait()
        row, col = iota((16, tabv.shape[0]), 0), iota((16, tabv.shape[0]), 1)
        wanted = jnp.where(row == 0, ts[0], ts[1])
        hits = jnp.where(jnp.logical_and(col == wanted, row < 2), 1.0, 0.0).astype(BF)
        picked = mm(hits, tabv[...])
        for i in range(2):
            embs[i] = jnp.broadcast_to(picked[i : i + 1], (16, width)).astype(BF)
        swap_start(lambda i: embs.at[i], lambda s: embr.at[s], esend, erecv)
        for s in range(2):
            swap_wait(lambda s: embr.at[s], erecv, s)
        gain, shift = row_of(gains, 0), row_of(shifts, 0)
        for s in range(2):
            swap_wait(x_at, xrecv, s)
            emb = embr[s][0:1, :].astype(F32)

            @pl.loop(0, part // 128)
            def _(b):
                rows = pl.ds(pl.multiple_of(s * part + b * 128, 128), 128)
                unit, _ = norm_parts(xr[rows, :].astype(F32) + emb)
                low1[rows, :] = (unit * gain + shift).astype(BF)

        swap_start(lambda i: cot.at[i], c_at, csend, crecv)
        load(1, wm, wmv).wait()

        @pl.loop(0, PAIRS // 2)
        def _(i):
            res = mm(low1[...], wmv[:, at(i, 6 * PAIR)])
            for j in range(2):
                p = 2 * i + j
                t0, t1, t2 = (res[:, (3 * j + n) * PAIR : (3 * j + n + 1) * PAIR] for n in range(3))
                q2[p] = (jnp.where(low_half, t0, t1).astype(BF) * 0.125).astype(BF)
                kv[p, 0, mine, :] = pltpu.roll(jnp.where(low_half, t2, t0), HEAD_SIZE, 1).astype(BF)
                kv[p, 1, mine, :] = jnp.where(low_half, t1, t2).astype(BF)
                kv_copy(p).start()

    def attend():
        @pl.loop(0, PAIRS)
        def _(p):
            kv_copy(p).wait_recv()
            q, keys, vals = q2[p], kv[p, 0], kv[p, 1]
            scores = [mm_nt(jnp.where(half, q, jnp.zeros_like(q)), keys) for half in (low_half, high_half)]
            tops = [jnp.max(s, axis=-1, keepdims=True) for s in scores]
            powers = [jnp.exp(s - top) for s, top in zip(scores, tops)]
            lows = [e.astype(BF) for e in powers]
            totals = [jnp.sum(e, axis=-1, keepdims=True) for e in powers]
            outs = [mm(e, vals) * (1.0 / total) for e, total in zip(lows, totals)]
            sums = [top + jnp.log(total) for top, total in zip(tops, totals)]
            mixed[:, at(p, PAIR)] = jnp.where(low_half, *outs).astype(BF)
            ls[...] = jnp.where(lane == 2 * p, sums[0], jnp.where(lane == 2 * p + 1, sums[1], ls[...]))

        lst[...] = ls[...].T

    def feed(wov, wuv, wdv, mid, low2, low2t, hid, rl):
        load(2, wo, wov).wait()
        gain, shift, bias = row_of(gains, 1), row_of(shifts, 1), row_of(biases, 0)

        @pl.loop(0, 2)
        def _(b):
            rows = at(b, blk)
            v = xr[rows, :].astype(F32) + embr[b][0:1, :].astype(F32)
            v = v + mm(mixed[rows, :], wov[...]) + bias
            mid[rows, :] = v
            low2[rows, :] = (norm_parts(v)[0] * gain + shift).astype(BF)

        low2t[...] = low2[...].T
        load(3, wu, wuv).wait()

        @pl.loop(0, ff // STEP)
        def _(j):
            cols = at(j, STEP)
            r = mm(low2[...], wuv[:, cols]) + upv[:, cols]
            half = 0.5 * (1.0 + lax.erf(r * math.sqrt(0.5)))
            bell = jnp.exp(r * r * -0.5) * (1.0 / math.sqrt(2.0 * math.pi))
            hid[:, cols] = (r * half).astype(BF)
            rl[:, cols] = (half + r * bell).astype(BF)

        load(4, wd, wdv).wait()
        for s in range(2):
            swap_wait(c_at, crecv, s)
        n = g.shape[-2]

        @pl.loop(0, 4)
        def _(j):
            res = mm_tn(hid[:, at(j, width)], cr[...]).astype(BF)
            for s in range(2):
                for i in range(4):
                    first = (4 * s + i) * n
                    g[i, lax.div(j, 2), lax.rem(j, 2), s] = res[first : first + n]

        for i in range(4):
            units[i].start()
        fin = mid[...] + mm(hid[...], wdv[...]) + row_of(biases, 1)
        lov[...] = fin.astype(BF)
        sm[0, 8:9, :] = jnp.sum(fin * fin, axis=0, keepdims=True)
        point()

        @pl.loop(0, ff // STEP)
        def _(j):
            cols = at(j, STEP)
            low = (mm_nt(cr[...], wdv[cols, :]) * rl[:, cols].astype(F32)).astype(BF)
            rl[:, cols] = low
            upg[:, cols] = jnp.sum(low.astype(F32), axis=0, keepdims=True)
            points(4, j)


        @pl.loop(0, 4)
        def _(j):
            res = mm(low2t[...], rl[:, at(j, width)]).astype(BF)
            for i in range(8):
                g[4 + j, i // 4, (i // 2) % 2, i % 2] = res[i * n : (i + 1) * n]
            for i in range(4):

                @pl.when(j == i)
                def _():
                    units[4 + i].start()

            points(4, j)

        gm[...] = mm_nt(rl[...], wuv[...])
        point()

        @pl.loop(0, toks // 128)
        def _(b):
            rows = at(b, 128)
            unit, inv = norm_parts(mid[rows, :])
            raw = gm[rows, :]
            ct = cr[rows, :].astype(F32)
            grad = ct + norm_back(raw, unit, inv, gain)
            gm[rows, :] = grad
            sm[0, 0:1, :] += jnp.sum(raw * unit, axis=0, keepdims=True)
            sm[0, 1:2, :] += jnp.sum(raw, axis=0, keepdims=True)
            sm[0, 2:3, :] += jnp.sum(grad.astype(BF).astype(F32), axis=0, keepdims=True)
            sm[0, 3:4, :] += jnp.sum(ct, axis=0, keepdims=True)

        for i in range(4):
            sm[0, 4 + i : 5 + i, :] = upg[:, i * width : (i + 1) * width]
        point()
        res = mm_tn(mixed[...], gm[...].astype(BF)).astype(BF)
        for i in range(8):
            g[8, i // 4, (i // 2) % 2, i % 2] = res[i * n : (i + 1) * n]
        units[8].start()
        point()
        fold = lax.div(iota((PAIR, width), 1), HEAD_SIZE) == iota((PAIR, width), 0)
        fold = jnp.where(fold, 1.0, 0.0).astype(BF)
        dout = mm_nt(gm[...].astype(BF), wov[...]).astype(BF)
        do[...] = dout
        prod = dout.astype(F32) * mixed[...].astype(F32)
        high = prod.astype(BF)
        rest = (prod - high.astype(F32)).astype(BF)
        dt[...] = mm_nt(fold, high) + mm_nt(fold, rest)
        point()

    def forward(wov, wuv, wdv):
        load(2, wo, wov).start()
        load(3, wu, wuv).start()
        load(4, wd, wdv).start()
        sm[0] = jnp.zeros_like(sm[0])
        pl.run_scoped(project, pltpu.VMEM(wm.shape, BF), pltpu.VMEM(table.shape, BF))
        attend()
        pl.run_scoped(
            functools.partial(feed, wov, wuv, wdv),
            pltpu.VMEM((toks, width), F32), pltpu.VMEM((toks, width), BF), pltpu.VMEM((width, toks), BF),
            pltpu.VMEM((toks, ff), BF), pltpu.VMEM((toks, ff), BF),
        )

    pl.run_scoped(forward, pltpu.VMEM(wo.shape, BF), pltpu.VMEM(wu.shape, BF), pltpu.VMEM(wd.shape, BF))

    def backward(wmv, low1t, late_g, dkvs, dqa, dqkv, igv):
        load(5, wm, wmv).start()
        low1t[...] = low1[...].T
        for i in range(EARLY, UNITS):
            units[i] = Reduction(i, KINDS[i], late_g.at[i - EARLY], refs, outer)
        i_at = lambda s: igv.at[at(s, part)]

        def dkv_copy(p):
            return pltpu.make_async_remote_copy(
                dkvs.at[p], dkvr.at[p], dsend.at[p], drecv.at[p],
                device_id=(partner, z), device_id_type=MESH,
            )

        halves = (low_half, high_half)

        def attend_back(p, base):
            rows = pl.ds(pl.multiple_of(base, toks), toks)
            keys, vals = kv[p, 0, rows, :], kv[p, 1, rows, :]
            q, dout = q2[p], do[:, at(p, PAIR)]
            dks, dvs, dqs = [], [], []
            for h, half in enumerate(halves):
                kh = jnp.where(half, keys, jnp.zeros_like(keys))
                vh = jnp.where(half, vals, jnp.zeros_like(vals))
                probs = jnp.exp(mm_nt(kh, q) - lst[pl.ds(2 * p + h, 1), :])
                ds = (probs * (mm_nt(vh, dout) - dt[pl.ds(2 * p + h, 1), :])).astype(BF)
                dvs.append(mm(probs.astype(BF), dout))
                dks.append(mm(ds, q))
                dqs.append(mm_tn(ds, kh))
                if h == 0:
                    points(PAIRS, p)
            return jnp.where(low_half, *dks), jnp.where(low_half, *dvs), dqs[0] + dqs[1]

        @pl.loop(0, PAIRS)
        def _(p):
            dk, dv, dq = attend_back(p, (1 - c) * toks)
            dkvs[p, 0] = dk.astype(BF)
            dkvs[p, 1] = dv.astype(BF)
            dqa[...] = dq
            dkv_copy(p).start()
            points(PAIRS, p)
            dk, dv, dq = attend_back(p, c * toks)
            dkv_copy(p).wait_recv()
            dq = (dq + dqa[...]) * 0.125
            dk = pltpu.roll(dk + dkvr[p, 0].astype(F32), HEAD_SIZE, 1)
            dv = dv + dkvr[p, 1].astype(F32)
            dqkv[:, at(3 * p, PAIR)] = jnp.where(low_half, dq, dk).astype(BF)
            dqkv[:, at(3 * p + 1, PAIR)] = jnp.where(low_half, dv, dq).astype(BF)
            dqkv[:, at(3 * p + 2, PAIR)] = jnp.where(low_half, dk, dv).astype(BF)

            @pl.when(lax.rem(p, 2) == 1)
            def _():
                b = lax.div(p, 2)
                n = g.shape[-2]
                res = mm(low1t[...], dqkv[:, at(b, width)]).astype(BF)
                for j in range(8):
                    late_g[b, j // 4, (j // 2) % 2, j % 2] = res[j * n : (j + 1) * n]
                for i in range(3):

                    @pl.when(b == i)
                    def _():
                        units[EARLY + i].start()

            points(PAIRS, p)

        load(5, wm, wmv).wait()
        gain0 = row_of(gains, 0)
        here = 4 * k + z
        lanes = iota((1, width), 1)

        @pl.loop(0, 2)
        def _(b):
            rows = at(b, blk)
            raw = mm_nt(dqkv[rows, :], wmv[...])
            unit, inv = norm_parts(xr[rows, :].astype(F32) + embr[b][0:1, :].astype(F32))
            grad = gm[rows, :] + norm_back(raw, unit, inv, gain0)
            igv[rows, :] = grad.astype(BF)
            sm[0, 11:12, :] += jnp.sum(raw * unit, axis=0, keepdims=True)
            sm[0, 12:13, :] += jnp.sum(raw, axis=0, keepdims=True)
            sm[0, 13:14, :] += jnp.sum(grad, axis=0, keepdims=True)

        square = jnp.sum(sm[0, 8:9, :]) * (1.0 / (2 * toks * width))
        sm[0, 8:9, :] = jnp.where(lanes == here, square, 0.0)
        for row, source in ((9, ts), (10, buckets)):
            first, second = source[0].astype(F32), source[1].astype(F32)
            line = jnp.where(lanes == 2 * d, first, jnp.where(lanes == 2 * d + 1, second, 0.0))
            sm[0, row : row + 1, :] = jnp.where(z == 0, line, jnp.zeros_like(line))
        sums = sm.shape[1] - HEAD_ROWS
        sm[0, HEAD_ROWS:, :] = jnp.where(iota((sums, 1), 0) == here, sm[0, 13:14, :], 0.0)
        stages = [(flip(d, bit), z) for bit in bits] + [(d, flip(z, 1)), (d, flip(z, 2))]

        vectors = VectorSum(sm, sr, ssend, srecv, stages)
        units[VECTORS] = vectors
        for i in range(2):
            units[GRAD + i] = Return(i, i_at, lambda s: ihome.at[s], isend, irecv)
        vectors.start()

        def put(i):
            return pltpu.make_async_copy(f.at[i], f_out.at[i], osem.at[i])

        point()
        for one, stage in TAIL:
            units[one].take(stage)
            if one < UNITS and units[one].ends(stage):
                put(one).start()
        for one in range(UNITS):
            if not any(i == one and units[one].ends(stage) for i, stage in TAIL):
                put(one).start()
        extra = len(stages) - 5
        for i in range(extra):
            vectors.take(5 + i)
        result = pltpu.make_async_copy(sm.at[len(stages) % 2], total_out, wsem.at[0])
        result.start()
        for i in range(UNITS + 1):
            units[i].close()
        for i in range(UNITS):
            put(i).wait()
        result.wait()

        @pl.loop(0, PAIRS)
        def _(p):
            kv_copy(p).wait_send()
            dkv_copy(p).wait_send()

        for s in range(2):
            swap_wait(lambda s: lhome.at[s], lrecv, s)
            swap_wait(lambda s: ihome.at[s], irecv, s)
        swap_sent(lambda i: x.at[i], x_at, xsend, xrecv)
        swap_sent(lambda i: cot.at[i], c_at, csend, crecv)
        swap_sent(lambda i: embs.at[i], lambda s: embr.at[s], esend, erecv)
        swap_sent(l_at, lambda s: lhome.at[s], lsend, lrecv)
        swap_sent(i_at, lambda s: ihome.at[s], isend, irecv)

    shard = g.shape[-2]
    pl.run_scoped(
        backward,
        pltpu.VMEM(wm.shape, BF), pltpu.VMEM((width, toks), BF),
        pltpu.VMEM((UNITS - EARLY, 2, 2, 2, shard, width), BF), pltpu.VMEM((PAIRS, 2, toks, PAIR), BF),
        pltpu.VMEM((toks, PAIR), F32), pltpu.VMEM((toks, 3 * width), BF),
        pltpu.VMEM((toks, width), BF),
    )


def run_layer(ts, buckets, x, cot, table, wm, wo, wu, wd, gains, shifts, biases, upb, dp):
    _, part, width = x.shape
    toks = 2 * part
    ff = wu.shape[1]
    shard = width // 8
    bits = axis_bits(dp)
    rows = HEAD_ROWS + 2 * dp
    stages = len(bits) + 2
    vm = lambda shape, dtype: pltpu.VMEM(shape, dtype)
    any_ = pl.BlockSpec(memory_space=pl.ANY)
    vmem = pl.BlockSpec(memory_space=pltpu.VMEM)
    smem = pl.BlockSpec(memory_space=pltpu.SMEM)
    dma = lambda *n: pltpu.SemaphoreType.DMA(n)
    return pl.pallas_call(
        functools.partial(layer_kernel, bits),
        out_shape=(
            sds((2, part, width), BF), sds((2, part, width), BF), sds((UNITS, shard, width), BF),
            sds((rows, width), F32),
        ),
        in_specs=[smem] * 2 + [any_] * 7 + [vmem] * 4,
        out_specs=(any_,) * 4,
        scratch_shapes=[
            vm((toks, width), BF), vm((toks, width), BF), vm((2, 16, width), BF), vm((2, 16, width), BF),
            vm((PAIRS, 2, 2 * toks, PAIR), BF), vm((PAIRS, 2, toks, PAIR), BF),
            vm((UNITS, 2, 2, shard, width), BF), vm((UNITS, 2, shard, width), BF), vm((UNITS, shard, width), BF),
            vm((UNITS, shard // 2, width), BF), vm((UNITS, shard // 2, width), BF),
            vm((UNITS, shard, width), BF), vm((2, rows, width), F32), vm((stages, rows, width), F32),
            vm((toks, width), BF), vm((PAIRS, toks, PAIR), BF), vm((toks, width), BF), vm((toks, width), BF),
            vm((toks, width), F32), vm((toks, width), BF), vm((EARLY, 2, 2, 2, shard, width), BF),
            vm((toks, PAIR), F32), vm((PAIR, toks), F32), vm((PAIR, toks), F32), vm((1, ff), F32), vm((1, ff), F32),
            dma(2), dma(2), dma(2), dma(2), dma(2), dma(2), dma(PAIRS), dma(PAIRS),
            dma(2), dma(2), dma(2), dma(2), dma(PAIRS), dma(PAIRS), dma(UNITS, 10), dma(UNITS, 10),
            dma(stages), dma(stages), dma(6), dma(UNITS),
        ],
        compiler_params=pltpu.CompilerParams(
            collective_id=0, has_side_effects=True, vmem_limit_bytes=127 << 19
        ),
        cost_estimate=pl.CostEstimate(
            flops=32_000_000_000, bytes_accessed=60_000_000, transcendentals=20_000_000
        ),
        name="layer",
    )(ts, buckets, x, cot, table, wm, wo, wu, wd, gains, shifts, biases, upb)


def finish_kernel(
    lhome, ihome_in, f_in, total_in, *refs,
):
    big, small, held = refs[:7], refs[7:13], refs[13:20]
    layer_out, input_grad, mixer, output, up, down, table = held
    gains, shifts, biases, upb, norms, counts = small
    ihome, f, total, sem, done = refs[20:]
    n, width = f.shape[1:]
    columns, step_count = table.shape
    copies = [pltpu.make_async_copy(total_in, total, sem.at[0])]
    copies += [
        pltpu.make_async_copy(f_in.at[pl.ds(4 * i, 4)], f.at[pl.ds(4 * i, 4)], sem.at[1 + i]) for i in range(3)
    ]
    copies += [pltpu.make_async_copy(ihome_in, ihome, sem.at[4]), pltpu.make_async_copy(lhome, layer_out, sem.at[5])]
    for one in copies:
        one.start()
    leave = [pltpu.make_async_copy(src, dst, done.at[i]) for i, (src, dst) in enumerate(zip(held, big))]
    copies[1].wait()
    for i in range(4):
        down[i * n : (i + 1) * n, :] = f[i].astype(F32)
    leave[5].start()
    copies[2].wait()
    for i in range(4):
        up[:, i * width : (i + 1) * width] = f[4 + i].astype(F32)
    leave[4].start()
    copies[4].wait()
    input_grad[...] = ihome[...].astype(F32)
    leave[1].start()
    copies[3].wait()
    output[...] = f[8].astype(F32)
    for i in range(3):
        mixer[:, i * width : (i + 1) * width] = f[9 + i].astype(F32)
    leave[3].start()
    leave[2].start()
    copies[5].wait()
    leave[0].start()
    copies[0].wait()
    for i in range(4):
        upb[pl.ds(i * width, width)] = total[4 + i, :]
    for i, row in enumerate((11, 0)):
        gains[i : i + 1, :] = total[row : row + 1, :]
        shifts[i : i + 1, :] = total[row + 1 : row + 2, :]
    biases[...] = total[2:4, :]
    count = total.shape[0] - HEAD_ROWS
    first = lax.axis_index("dp") * columns
    chosen = iota((width, columns), 0) == iota((width, columns), 1) + first
    chosen = jnp.where(chosen, 1.0, 0.0).astype(BF)
    steps = total[9:10, :count]
    hits = jnp.where(iota((step_count, count), 0).astype(F32) == steps, 1.0, 0.0).astype(BF)
    here = iota((BUCKETS, count), 0).astype(F32) == total[10:11, :count]
    here = jnp.where(here, 1.0, 0.0).astype(BF)
    rest, grad = total[HEAD_ROWS:, :], 0.0
    means = jnp.where(iota((8, count), 0) == 0, total[8:9, :count], 1.0)
    norm = 0.0
    for _ in range(3):
        piece = rest.astype(BF)
        rest = rest - piece.astype(F32)
        part = mm(piece, chosen).astype(BF)
        grad = grad + lax.dot_general(part, hits, (((0,), (1,)), ((), ())), preferred_element_type=F32)
        piece = means.astype(BF)
        means = means - piece.astype(F32)
        norm = norm + mm_nt(piece, here)
    table[...] = grad
    leave[6].start()
    norms[...] = norm[0, :]
    counts[...] = norm[1, :]
    for one in leave:
        one.wait()


def run_finish(lhome, ihome, f, total, dp, steps):
    n, width = f.shape[1:]
    big = [
        sds(lhome.shape, BF), sds(ihome.shape, F32), sds((n, 3 * width), F32), sds((n, width), F32),
        sds((n, 4 * width), F32), sds((4 * n, width), F32), sds((width // dp, steps), F32),
    ]
    small = [sds((2, width), F32)] * 3 + [sds((4 * width,), F32), sds((BUCKETS,), F32), sds((BUCKETS,), F32)]
    vmem, any_ = pl.BlockSpec(memory_space=pltpu.VMEM), pl.BlockSpec(memory_space=pl.ANY)
    res = pl.pallas_call(
        finish_kernel,
        out_shape=big + small,
        in_specs=[any_] * 4,
        out_specs=[any_] * len(big) + [vmem] * len(small),
        scratch_shapes=[pltpu.VMEM(one.shape, one.dtype) for one in big] + [
            pltpu.VMEM(ihome.shape, BF), pltpu.VMEM(f.shape, f.dtype), pltpu.VMEM(total.shape, F32),
            pltpu.SemaphoreType.DMA((6,)), pltpu.SemaphoreType.DMA((len(big),)),
        ],
        compiler_params=pltpu.CompilerParams(vmem_limit_bytes=60 << 20),
        name="finish",
    )(lhome, ihome, f, total)
    return (*res[:6], *res[7:11], res[6].T, *res[11:])


def body(
    inputs, cotangent, time_table, timesteps, buckets, mixer_weight, output_weight, up_weight, down_weight,
    norm_gain, norm_shift, output_bias, up_bias,
):
    width = inputs.shape[-1]
    dp = lax.axis_size("dp")
    lhome, ihome, shares, total = run_layer(
        timesteps, buckets, inputs, cotangent, time_table, mixer_weight, output_weight, up_weight,
        down_weight, norm_gain, norm_shift, output_bias, up_bias, dp,
    )
    inner = dp // 8
    if inner > 1:
        teams = [[h * inner + i for i in range(inner)] for h in range(8)]
        scatter = lambda a, axis: lax.psum_scatter(
            a, "dp", scatter_dimension=axis, axis_index_groups=teams, tiled=True
        )
        shares = shares.astype(F32)
        down, rest = scatter(shares[0:4].reshape(width // 2, width), 0), scatter(shares[4:UNITS], 1)
        shares = jnp.concatenate([down.reshape((4,) + rest.shape[1:]), rest])
    return run_finish(lhome, ihome, shares, total, dp, time_table.shape[0])


def solution(mesh):
    tokens = P("dp", "seq", None)
    return jax.shard_map(
        body,
        mesh=mesh,
        in_specs=(tokens, tokens, P(), P("dp"), P("dp")) + (P(),) * 8,
        out_specs=(tokens, tokens) + (P("dp", None),) * 4 + (P(),) * 4 + (P(None, "dp"), P(), P()),
        check_vma=False,
    )
```
